512 devices in a mesh: frame: 32 (over z, y_lo, core), orient: 4 (over x), pix: 4 (over y_hi).
Axes of the slice: x: 4, y: 8 (y_hi: 4, y_lo: 2; y = y_hi * 2 + y_lo), z: 8, core: 2. Of those that a mesh axis runs over, the one named last changes fastest.
Arguments:
- photon_counts: int32 [512, 16384], P('frame', 'pix'), may hold values from 0 to 8, as said below
- slices: bfloat16 [768, 16384], P('orient', 'pix'), may hold values from 0.049804688 to 2
- owner_ids: int32 [768, 128], P('orient', 'pix'), may hold values from 0 to 3
- tile_ids: int32 [768, 128], P('orient', 'pix'), may hold values from 0 to 2047
- patch_count: int32 [768], P('orient'), may hold values from 16 to 128
- old_model: float32 [1024, 128], P(('frame', 'orient', 'pix')), may hold values from 0.1 to 2
Outputs:
- orient_prob: bfloat16 [512, 768], P('frame', 'orient')
- merged: float32 [1024, 128], P(('frame', 'orient', 'pix'))
The draws below stay inside these ranges and needn't reach their ends.
Inputs may be any that keep to these rules, and one draw needn't show every extreme that they name: `photon_counts`: each frame's counts stay below a level of 3 to 9 drawn for that frame.
All inputs are finite; a program needn't handle non-finite values.
Results may differ from the reference program's by a relative error of at most 0.0029.
The reference program's roundings to bfloat16 on the way (of `log_slice` and `frames_bf`) count: a program that leaves them out, or rounds other values in their place, can miss the bound.
Values sent between devices are 32-bit elements; how exact they have to be, the bound alone decides.
A program may use at most 64 MiB of HBM per device.

```python
import math
import jax
import jax.numpy as jnp
from jax import lax

P_SIZE = 16384
R = 768
NB = 4
BRICK_ROWS = 256
SHIFTS = 8
FRAMES = 512
NQ = 128
MROWS = 1024


def draw_photon_counts(key, part):
    first_key, second_key = jax.random.split(jax.random.fold_in(key, 11))
    level = jax.random.randint(first_key, (FRAMES, 1), 3, 10)
    return jax.random.randint(second_key, (FRAMES, P_SIZE), 0, level).astype(jnp.int32)


def touch_ends(entries, stream_key, low, top_value):
    spot = [jax.random.randint(jax.random.fold_in(stream_key, axis), (), 0, length) for axis, length in enumerate(entries.shape)]
    widest = entries.shape.index(max(entries.shape))
    neighbour = spot[:widest] + [(spot[widest] + 1) % entries.shape[widest]] + spot[widest + 1:]
    return entries.at[tuple(spot)].set(low).at[tuple(neighbour)].set(top_value)


def level_of(key, dims, cuts, least, largest):
    loudness = 1.0
    for axis_at, parts in cuts:
        draws = jax.random.uniform(jax.random.fold_in(jax.random.fold_in(key, 6), axis_at), (parts,), jnp.float32, least / len(cuts), largest / len(cuts))
        loudness = loudness * jnp.repeat(jnp.exp(draws), dims[axis_at] // parts).reshape((-1,) + (1,) * (len(dims) - 1 - axis_at))
    return loudness


def setup_inputs(seed: int = 0) -> dict:
    seeds = jax.random.split(jax.random.key(seed), 7)
    return {
        "photon_counts": draw_photon_counts(jax.random.fold_in(seeds[6], 71), 0),
        "slices": jnp.clip(jnp.exp(math.log(2.0) - 3.6927934 * jax.random.uniform(seeds[1], (R, P_SIZE), jnp.float32) ** level_of(seeds[1], (R, P_SIZE), ((0, 4), (1, 4)), -0.2, 0.2)), 0.049804688, 2.0).astype(jnp.bfloat16),
        "owner_ids": touch_ends(jax.random.randint(seeds[2], (R, NQ), 0, NB), jax.random.fold_in(seeds[2], 1), 0, NB - 1).astype(jnp.int32),
        "tile_ids": touch_ends(jax.random.randint(seeds[3], (R, NQ), 0, BRICK_ROWS * SHIFTS), jax.random.fold_in(seeds[3], 1), 0, (BRICK_ROWS * SHIFTS) - 1).astype(jnp.int32),
        "patch_count": touch_ends(jax.random.randint(seeds[4], (R,), NQ // 8, NQ + 1), jax.random.fold_in(seeds[4], 1), NQ // 8, NQ).astype(jnp.int32),
        "old_model": jnp.clip(jnp.exp(math.log(2.0) - 2.9957323 * jax.random.uniform(seeds[5], (MROWS, 128), jnp.float32) ** level_of(seeds[5], (MROWS, 128), ((0, 512),), -0.2, 0.2)), 0.1, 2.0),
    }


def deposit(values, weights, owners, tile_ids, live_mask, rows_total):
    shift_ids = tile_ids % SHIFTS
    row_index = owners * BRICK_ROWS + tile_ids // SHIFTS
    lanes = lax.iota(jnp.int32, 128)
    lane_index = (lanes[None, None, :] - 17 * shift_ids[:, :, None]) % 128
    moved = jnp.take_along_axis(values, lane_index, axis=2) * live_mask[:, :, None]
    flat_rows = row_index.reshape(-1)
    brick_sum = jnp.zeros((rows_total, 128), jnp.float32).at[flat_rows].add(moved.reshape(-1, 128))
    brick_weight = jnp.zeros((rows_total,), jnp.float32).at[flat_rows].add((live_mask * weights[:, None]).reshape(-1))
    return (brick_sum, brick_weight)

def reference(photon_counts, slices, owner_ids, tile_ids, patch_count, old_model):
    frames_bf = photon_counts.astype(jnp.bfloat16)
    log_slice = jnp.log(slices.astype(jnp.float32)).astype(jnp.bfloat16)
    fit = jnp.dot(frames_bf, log_slice.T, preferred_element_type=jnp.float32)
    slice_mass = lax.optimization_barrier(jnp.sum(slices.astype(jnp.float32), axis=1))
    score = (fit - slice_mass[None, :]) * (1.0 / math.sqrt(P_SIZE))
    score_top = lax.optimization_barrier(jnp.max(score, axis=1))
    weights_exp = jnp.exp(score - score_top[:, None])
    score_total = lax.optimization_barrier(jnp.sum(weights_exp, axis=1))
    orient_prob = (weights_exp / score_total[:, None]).astype(jnp.bfloat16)
    total_weight = lax.optimization_barrier(jnp.sum(orient_prob.astype(jnp.float32), axis=0))
    photon_sum = jnp.dot(orient_prob.T, frames_bf, preferred_element_type=jnp.float32)
    patch_id = lax.iota(jnp.int32, NQ)
    live_mask = (patch_id[None, :] < patch_count[:, None]).astype(jnp.float32)
    brick_sum, brick_weight = deposit(photon_sum.reshape(R, NQ, 128), total_weight, owner_ids, tile_ids, live_mask, MROWS)
    prior = FRAMES * NQ / (4.0 * MROWS)
    merged = (brick_sum + prior * old_model) / (brick_weight[:, None] + prior)
    return (orient_prob, merged)
```

```python
import functools
import math

import jax
import jax.numpy as jnp
from jax import lax
from jax.experimental import pallas as pl
from jax.experimental.pallas import tpu as pltpu
from jax.sharding import PartitionSpec as P

XN, YN, ZN = 4, 8, 8
PEERS_X = XN - 1
PIXELS = 16384
SHIFTS = 8
PRIOR = 512 * 128 / (4.0 * 1024)
ROWS = 512
KTOT = 192 * 32
F32 = jnp.float32
BF16 = jnp.bfloat16
NT = (((1,), (1,)), ((), ()))


def lanes(shape):
    return lax.broadcasted_iota(jnp.int32, shape, len(shape) - 1)


def sublanes(shape):
    return lax.broadcasted_iota(jnp.int32, shape, len(shape) - 2)


def kernel(
    counts_in, slices_in, owner_in, tile_in, count_in, old_in,
    prob_out, merged_out,
    cnt, pcnt, sl, own_v, til_v, pc_v, old_v,
    idpad, fit_scr, shm_scr, rep_scr, wsel_scr, grolled, rowk, ohs, rhs,
    psend, precv, ssend, srecv, ppart,
    xs, xr, asd, ar, bsd, br,
    loc_sem, fr_send, fr_recv, p_send, p_recv, s_send, s_recv, x_send, x_recv, a_send, a_recv, b_send, b_recv,
):
    fi = lax.axis_index("frame")
    x = lax.axis_index("orient")
    y_hi = lax.axis_index("pix")
    z = fi // 4
    y_lo = (fi // 2) % 2
    core = fi % 2
    y = y_hi * 2 + y_lo
    swap = 1 - core

    def place(xx, yy, zz, cc):
        return {"frame": zz * 4 + (yy % 2) * 2 + cc, "orient": xx, "pix": yy // 2}

    locals_ = [
        pltpu.make_async_copy(counts_in, cnt, loc_sem.at[0]),
        *[
            pltpu.make_async_copy(
                slices_in.at[:, c * 1024 : (c + 1) * 1024], sl.at[:, c * 1024 : (c + 1) * 1024], loc_sem.at[1 + c]
            )
            for c in range(4)
        ],
        pltpu.make_async_copy(owner_in, own_v, loc_sem.at[5]),
        pltpu.make_async_copy(tile_in, til_v, loc_sem.at[6]),
        pltpu.make_async_copy(count_in, pc_v, loc_sem.at[7]),
        pltpu.make_async_copy(old_in, old_v, loc_sem.at[8]),
    ]
    for copy in locals_:
        copy.start()

    barrier = pltpu.get_barrier_semaphore()
    pl.semaphore_signal(barrier, inc=1, device_id=place(x, y, z, swap))
    for d in range(1, XN):
        for cc in (core, swap):
            pl.semaphore_signal(barrier, inc=1, device_id=place((x + d) % XN, y, z, cc))
    for d in range(1, YN):
        pl.semaphore_signal(barrier, inc=1, device_id=place(x, (y + d) % YN, z, core))
    for d in range(1, ZN):
        pl.semaphore_signal(barrier, inc=1, device_id=place(x, y, (z + d) % ZN, core))

    locals_[0].wait()
    fit = jnp.zeros((16, 192), F32)
    mass = jnp.zeros((192, 128), F32)
    for c in range(16):
        if c % 4 == 0:
            locals_[1 + c // 4].wait()
        s32 = sl[:, c * 256 : (c + 1) * 256].astype(F32)
        mass = mass + (s32[:, :128] + s32[:, 128:])
        fr = cnt[:, c * 256 : (c + 1) * 256].astype(F32).astype(BF16)
        fit = fit + lax.dot_general(fr, jnp.log(s32).astype(BF16), NT, preferred_element_type=F32)
    fit = fit - lax.dot_general(
        jnp.ones((16, 128), F32), mass, NT, precision=lax.Precision.HIGHEST, preferred_element_type=F32
    )
    fit_scr[...] = jnp.zeros((16, 256), F32)
    fit_scr[:, 0:192] = fit
    lane8 = lanes((8, 128))
    psend[0:16, :] = fit_scr[:, 0:128]
    psend[16:24, :] = jnp.where(lane8 < 64, fit_scr[0:8, 128:256], pltpu.roll(fit_scr[8:16, 128:256], 64, 1))

    pl.semaphore_wait(barrier, 1 + 2 * PEERS_X + (YN - 1) + (ZN - 1))

    p_copies = [
        pltpu.make_async_remote_copy(
            psend, precv.at[d - 1], p_send.at[d - 1], p_recv.at[d - 1],
            device_id=place(x, (y + 2 * d) % YN, z, core),
        )
        for d in range(1, 4)
    ]
    for copy in p_copies:
        copy.start()
    swap_frames = pltpu.make_async_remote_copy(
        cnt, pcnt, fr_send.at[0], fr_recv.at[0], device_id=place(x, y, z, swap)
    )
    swap_frames.start()

    for copy in locals_[5:]:
        copy.wait()
    tid = til_v[...]
    rid = own_v[...] * 256 + (tid >> 3)
    ry = ((rid >> 1) & 3) * 2 + ((rid >> 6) & 1)
    rz = rid >> 7
    spot = ((rid >> 3) & 3) * 128 + (ry * swap + rz * core) * 16 + (rz * swap + ry * core) * 2 + (rid & 1)
    spot = jnp.where(((rid >> 5) & 1) == core, spot, -1)
    idpad[...] = jnp.zeros((256, 128), jnp.int32)
    idpad[0:192, 0:32] = spot
    turned = jnp.transpose(idpad[...])
    rowk[0:32, :] = turned[0:32, 0:128]
    rowk[32:48, :] = jnp.where(
        lanes((16, 128)) < 64, turned[0:16, 128:256], pltpu.roll(turned[16:32, 128:256], 64, 1)
    )
    eye = (sublanes((192, 192)) == lanes((192, 192))).astype(F32).astype(BF16)
    pc_col = lax.dot_general(
        eye, jnp.broadcast_to(pc_v[...].astype(F32), (128, 192)).astype(BF16), NT, preferred_element_type=F32
    )
    shm_scr[...] = jnp.full((192, 128), float(SHIFTS), F32)
    live = (lanes((192, 32)) + y_hi * 32).astype(F32) < pc_col[:, 0:32]
    shm_scr[:, 0:32] = jnp.where(live, (tid & 7).astype(F32), float(SHIFTS))

    def roll_frames(source, half):
        def body(q, _):
            tile = source[:, pl.ds(pl.multiple_of(q * 128, 128), 128)].astype(F32)
            for s in range(SHIFTS):
                moved = pltpu.roll(tile, 17 * s, 1) if s else tile
                grolled[q, half * 128 + s * 16 : half * 128 + (s + 1) * 16, :] = moved.astype(BF16)
            return 0

        lax.fori_loop(0, 32, body, 0, unroll=4)

    def onehot(first, last):
        def body(kb, _):
            line = jnp.broadcast_to(rowk[pl.ds(kb, 1), :], (128, 128))
            for b in range(4):
                hit = line == sublanes((128, 128)) + b * 128
                ohs[b * 128 : (b + 1) * 128, pl.ds(pl.multiple_of(kb * 128, 128), 128)] = jnp.where(
                    hit, 1.0, 0.0
                ).astype(BF16)
            return 0

        lax.fori_loop(first, last, body, 0, unroll=2)

    roll_frames(cnt, 0)
    onehot(0, 16)

    for copy in p_copies:
        copy.wait_recv()
    score = (psend[...] + precv[0] + precv[1] + precv[2]) * (1.0 / math.sqrt(PIXELS))
    score_a, tail = score[0:16], score[16:24]
    off = -3.0e38
    score_b = jnp.concatenate(
        [jnp.where(lane8 < 64, tail, off), jnp.where(lane8 < 64, pltpu.roll(tail, 64, 1), off)], axis=0
    )
    top = jnp.maximum(
        jnp.max(score_a, axis=1, keepdims=True), jnp.max(score_b, axis=1, keepdims=True)
    )
    exp_a = jnp.exp(score_a - top)
    exp_b = jnp.exp(score_b - top)
    total = jnp.sum(exp_a, axis=1, keepdims=True) + jnp.sum(exp_b, axis=1, keepdims=True)
    ssend[0:8, :] = jnp.where(
        lane8 < 64,
        jnp.where(lane8 < 32, top[0:8], total[0:8]),
        jnp.where(lane8 < 96, top[8:16], total[8:16]),
    )
    ssend[8:24, :] = exp_a
    ssend[24:32, :] = jnp.where(lane8 < 64, exp_b[0:8], pltpu.roll(exp_b[8:16], 64, 1))
    s_copies = []
    for d in range(1, XN):
        for rel, cc in enumerate((core, swap)):
            slot = (d - 1) * 2 + rel
            s_copies.append(
                pltpu.make_async_remote_copy(
                    ssend.at[0:8], srecv.at[slot], s_send.at[slot], s_recv.at[slot],
                    device_id=place((x + d) % XN, y, z, cc),
                )
            )
    s_copies.append(
        pltpu.make_async_remote_copy(
            ssend, ppart, s_send.at[6], s_recv.at[6], device_id=place(x, y, z, swap)
        )
    )
    for copy in s_copies:
        copy.start()

    swap_frames.wait_recv()
    roll_frames(pcnt, 1)
    onehot(16, 48)

    for copy in s_copies:
        copy.wait_recv()

    def probabilities(packed, others):
        stats = packed[0:8, :]
        every = [stats, *others]
        most = functools.reduce(jnp.maximum, every)
        scale = pltpu.roll(jnp.exp(stats - most), 32, 1)
        whole = stats * scale
        for other in others:
            whole = whole + other * pltpu.roll(jnp.exp(other - most), 32, 1)
        factor = scale / whole
        low, high = factor[:, 32:33], factor[:, 96:97]
        prob_a = jnp.concatenate([packed[8:16, :] * low, packed[16:24, :] * high], axis=0)
        tail = packed[24:32, :]
        prob_b = jnp.concatenate([tail * low, pltpu.roll(tail, 64, 1) * high], axis=0)
        return prob_a.astype(BF16), prob_b.astype(BF16)

    own_a, own_b = probabilities(ssend, [srecv[0], srecv[2], srecv[4]])
    her_a, her_b = probabilities(ppart, [srecv[1], srecv[3], srecv[5]])
    prob_out[:, 0:128] = own_a
    prob_out[:, 128:192] = own_b[:, 0:64]

    stack = jnp.concatenate(
        [
            jnp.concatenate([own_a, own_b], axis=1)] * SHIFTS + [
            jnp.concatenate([her_a, her_b], axis=1)] * SHIFTS,
        axis=0,
    )
    eye = (sublanes((192, 256)) == lanes((192, 256))).astype(F32).astype(BF16)
    rep = lax.dot_general(eye, stack, NT, preferred_element_type=F32)
    rep_scr[...] = rep
    lane_shift = (lanes((192, 256)) % 128) // 16
    weights = jnp.dot(
        jnp.where(lane_shift == 0, rep, 0.0).astype(BF16), jnp.ones((256, 128), BF16), preferred_element_type=F32
    )
    upper = weights.astype(BF16).astype(F32)
    wsel_scr[...] = jnp.where(lanes((192, 128)) < 64, upper, weights - upper)

    def patches(t4, _):
        columns = pltpu.roll(shm_scr[...], 128 - 4 * t4, 1)
        for u in range(4):
            t = t4 * 4 + u
            for h in range(2):
                q = t + 16 * h
                shift = jnp.broadcast_to(columns[:, u + 16 * h : u + 16 * h + 1], (192, 128))
                lane = ((lanes((192, 128)) % 128) // 16).astype(F32)
                same = shift == lane
                left = jnp.concatenate(
                    [
                        jnp.where(same, rep_scr[:, 0:128], 0.0).astype(BF16),
                        jnp.where(same, rep_scr[:, 128:256], 0.0).astype(BF16),
                    ],
                    axis=1,
                )
                moved = jnp.dot(left, grolled[q], preferred_element_type=F32).astype(BF16)
                weighed = jnp.where(shift < SHIFTS - 0.5, wsel_scr[...], 0.0).astype(BF16)
                both = jnp.concatenate([moved, weighed], axis=1)
                rhs[pl.ds(pl.multiple_of(q * 128, 128), 128), :] = both[0:128]
                rhs[pl.ds(pl.multiple_of(4096 + t * 128 + h * 64, 64), 64), :] = both[128:192]
        return 0

    lax.fori_loop(0, 4, patches, 0)

    diagonal = sublanes((128, 128)) == lanes((128, 128))

    def deposit(d, _):
        block = (x + d) % XN
        picked = ohs[pl.ds(pl.multiple_of(block * 128, 128), 128), :]
        total = jnp.dot(picked, rhs[...], preferred_element_type=F32)
        halves = total[:, 128:256]
        weighed = jnp.where(diagonal, halves + pltpu.roll(halves, 64, 1), 0.0)
        slot = d % XN
        xs[slot, 0:128, :] = total[:, 0:128]
        xs[slot, 128:136, :] = jnp.broadcast_to(jnp.sum(weighed, axis=0, keepdims=True), (8, 128))
        return 0

    x_copies = [
        pltpu.make_async_remote_copy(
            xs.at[d], xr.at[d - 1], x_send.at[d - 1], x_recv.at[d - 1],
            device_id=place((x + d) % XN, y, z, core),
        )
        for d in range(1, XN)
    ]
    for d in (2, 1, 3, 4):
        deposit(d, 0)
        if d < XN:
            x_copies[d - 1].start()
    for copy in x_copies:
        copy.wait_recv()
    brick = xs[0] + xr[0] + xr[1] + xr[2]

    first = y * swap + z * core
    second = z * swap + y * core
    for k in range(8):
        asd[k, 0:16, :] = brick[k * 16 : (k + 1) * 16]
        asd[k, 16:24, :] = brick[128:136]
    a_copies = [
        pltpu.make_async_remote_copy(
            asd.at[(first + d) % 8], ar.at[d - 1], a_send.at[d - 1], a_recv.at[d - 1],
            device_id=place(x, (y + swap * d) % YN, (z + core * d) % ZN, core),
        )
        for d in range(1, 8)
    ]
    for copy in a_copies:
        copy.start()
    for copy in a_copies:
        copy.wait_recv()
    lines = asd[first]
    for d in range(7):
        lines = lines + ar[d]

    sub8 = sublanes((8, 128))
    for k in range(8):
        tile = lines[8 * (k // 4) : 8 * (k // 4) + 8]
        turned = pltpu.roll(tile, 8 - 2 * (k % 4), 0) if k % 4 else tile
        bsd[k] = jnp.where(sub8 < 2, turned, lines[16:24])
    b_copies = [
        pltpu.make_async_remote_copy(
            bsd.at[(second + d) % 8], br.at[d - 1], b_send.at[d - 1], b_recv.at[d - 1],
            device_id=place(x, (y + core * d) % YN, (z + swap * d) % ZN, core),
        )
        for d in range(1, 8)
    ]
    for copy in b_copies:
        copy.start()
    for copy in b_copies:
        copy.wait_recv()
    last = bsd[second]
    for d in range(7):
        last = last + br[d]
    mine = lanes((2, 128)) == sublanes((2, 128)) + (first * 16 + second * 2)
    weight = jnp.sum(jnp.where(mine, last[2:4], 0.0), axis=1, keepdims=True)
    merged_out[...] = (last[0:2] + PRIOR * old_v[...]) / (weight + PRIOR)

    swap_frames.wait_send()
    for copy in (*p_copies, *s_copies, *x_copies, *a_copies, *b_copies):
        copy.wait_send()


def shards(photon_counts, slices, owner_ids, tile_ids, patch_count, old_model):
    dma = pltpu.SemaphoreType.DMA
    return pl.pallas_call(
        kernel,
        out_shape=(jax.ShapeDtypeStruct((16, 192), BF16), jax.ShapeDtypeStruct((2, 128), F32)),
        in_specs=[pl.BlockSpec(memory_space=pl.ANY)] * 6,
        out_specs=(pl.BlockSpec(memory_space=pltpu.VMEM), pl.BlockSpec(memory_space=pltpu.VMEM)),
        scratch_shapes=[
            pltpu.VMEM((16, 4096), jnp.int32),
            pltpu.VMEM((16, 4096), jnp.int32),
            pltpu.VMEM((192, 4096), BF16),
            pltpu.VMEM((192, 32), jnp.int32),
            pltpu.VMEM((192, 32), jnp.int32),
            pltpu.VMEM((1, 192), jnp.int32),
            pltpu.VMEM((2, 128), F32),
            pltpu.VMEM((256, 128), jnp.int32),
            pltpu.VMEM((16, 256), F32),
            pltpu.VMEM((192, 128), F32),
            pltpu.VMEM((192, 256), F32),
            pltpu.VMEM((192, 128), F32),
            pltpu.VMEM((32, 256, 128), BF16),
            pltpu.VMEM((48, 128), jnp.int32),
            pltpu.VMEM((ROWS, KTOT), BF16),
            pltpu.VMEM((KTOT, 256), BF16),
            pltpu.VMEM((24, 128), F32),
            pltpu.VMEM((3, 24, 128), F32),
            pltpu.VMEM((32, 128), F32),
            pltpu.VMEM((6, 8, 128), F32),
            pltpu.VMEM((32, 128), F32),
            pltpu.VMEM((4, 136, 128), F32),
            pltpu.VMEM((3, 136, 128), F32),
            pltpu.VMEM((8, 24, 128), F32),
            pltpu.VMEM((7, 24, 128), F32),
            pltpu.VMEM((8, 8, 128), F32),
            pltpu.VMEM((7, 8, 128), F32),
            dma((9,)),
            dma((1,)), dma((1,)),
            dma((3,)), dma((3,)),
            dma((7,)), dma((7,)),
            dma((3,)), dma((3,)),
            dma((7,)), dma((7,)),
            dma((7,)), dma((7,)),
        ],
        compiler_params=pltpu.CompilerParams(
            collective_id=0, has_side_effects=True, vmem_limit_bytes=40 * 1024 * 1024
        ),
        cost_estimate=pl.CostEstimate(flops=2 * 10**9, bytes_accessed=2 * 10**6, transcendentals=10**6),
        name="em_step",
    )(photon_counts, slices, owner_ids, tile_ids, patch_count.reshape(1, -1), old_model)


def solution(mesh):
    placed = (
        P("frame", "pix"),
        P("orient", "pix"),
        P("orient", "pix"),
        P("orient", "pix"),
        P("orient"),
        P(("frame", "orient", "pix"), None),
    )
    return jax.shard_map(
        shards,
        mesh=mesh,
        in_specs=placed,
        out_specs=(P("frame", "orient"), P(("frame", "orient", "pix"), None)),
        check_vma=False,
    )
```

```python
import functools
import math

import jax
import jax.numpy as jnp
from jax import lax
from jax.experimental import pallas as pl
from jax.experimental.pallas import tpu as pltpu
from jax.sharding import PartitionSpec as P

XN, YN, ZN = 4, 8, 8
FAR8 = (4, 3, 5, 2, 6, 1, 7)
FAR4 = (2, 1, 3, 0)
PIXELS = 16384
SHIFTS = 8
PRIOR = 512 * 128 / (4.0 * 1024)
ROWS = 512
KTOT = 192 * 32
F32 = jnp.float32
BF16 = jnp.bfloat16
NT = (((1,), (1,)), ((), ()))


def lanes(shape):
    return lax.broadcasted_iota(jnp.int32, shape, len(shape) - 1)


def sublanes(shape):
    return lax.broadcasted_iota(jnp.int32, shape, len(shape) - 2)


def kernel(
    counts_in, slices_in, owner_in, tile_in, count_in, old_in,
    prob_out, merged_out,
    cnt, pcnt, sl, own_v, til_v, pc_v, old_v,
    idpad, fit_scr, shm_scr, rep_scr, wsel_scr, grolled, rowk, ohs, rhs,
    psend, precv, ssend, srecv, ppart,
    xs, xr, bsd, br,
    loc_sem, fr_send, fr_recv, p_send, p_recv, s_send, s_recv, x_send, x_recv, b_send, b_recv,
):
    fi = lax.axis_index("frame")
    x = lax.axis_index("orient")
    y_hi = lax.axis_index("pix")
    z = fi // 4
    y_lo = (fi // 2) % 2
    core = fi % 2
    y = y_hi * 2 + y_lo
    swap = 1 - core

    def place(xx, yy, zz, cc):
        return {"frame": zz * 4 + (yy % 2) * 2 + cc, "orient": xx, "pix": yy // 2}

    def along_first(dx, df):
        return place((x + dx) % XN, (y + swap * df) % YN, (z + core * df) % ZN, core)

    locals_ = [
        pltpu.make_async_copy(counts_in, cnt, loc_sem.at[0]),
        *[
            pltpu.make_async_copy(
                slices_in.at[:, c * 1024 : (c + 1) * 1024], sl.at[:, c * 1024 : (c + 1) * 1024], loc_sem.at[1 + c]
            )
            for c in range(4)
        ],
        pltpu.make_async_copy(owner_in, own_v, loc_sem.at[5]),
        pltpu.make_async_copy(tile_in, til_v, loc_sem.at[6]),
        pltpu.make_async_copy(count_in, pc_v, loc_sem.at[7]),
        pltpu.make_async_copy(old_in, old_v, loc_sem.at[8]),
    ]
    for copy in locals_:
        copy.start()

    barrier = pltpu.get_barrier_semaphore()
    for d in FAR8:
        pl.semaphore_signal(barrier, inc=1, device_id=place(x, (y + core * d) % YN, (z + swap * d) % ZN, core))
    for df in (*FAR8, 0):
        for dx in FAR4:
            if dx or df:
                pl.semaphore_signal(barrier, inc=1, device_id=along_first(dx, df))
    for d in FAR4[:3]:
        pl.semaphore_signal(barrier, inc=1, device_id=place((x + d) % XN, y, z, swap))
    pl.semaphore_signal(barrier, inc=1, device_id=place(x, y, z, swap))

    locals_[0].wait()
    fit = jnp.zeros((16, 192), F32)
    mass = jnp.zeros((192, 128), F32)
    for c in range(16):
        if c % 4 == 0:
            locals_[1 + c // 4].wait()
        s32 = sl[:, c * 256 : (c + 1) * 256].astype(F32)
        mass = mass + (s32[:, :128] + s32[:, 128:])
        fr = cnt[:, c * 256 : (c + 1) * 256].astype(F32).astype(BF16)
        fit = fit + lax.dot_general(fr, jnp.log(s32).astype(BF16), NT, preferred_element_type=F32)
    fit = fit - lax.dot_general(
        jnp.ones((16, 128), F32), mass, NT, precision=lax.Precision.HIGHEST, preferred_element_type=F32
    )
    fit_scr[...] = jnp.zeros((16, 256), F32)
    fit_scr[:, 0:192] = fit
    lane8 = lanes((8, 128))
    psend[0:16, :] = fit_scr[:, 0:128]
    psend[16:24, :] = jnp.where(lane8 < 64, fit_scr[0:8, 128:256], pltpu.roll(fit_scr[8:16, 128:256], 64, 1))

    pl.semaphore_wait(barrier, 7 + 31 + 3 + 1)

    p_copies = [
        pltpu.make_async_remote_copy(
            psend, precv.at[d - 1], p_send.at[d - 1], p_recv.at[d - 1],
            device_id=place(x, (y + 2 * d) % YN, z, core),
        )
        for d in (2, 1, 3)
    ]
    for copy in p_copies:
        copy.start()
    swap_frames = pltpu.make_async_remote_copy(
        cnt, pcnt, fr_send.at[0], fr_recv.at[0], device_id=place(x, y, z, swap)
    )
    swap_frames.start()

    for copy in locals_[5:]:
        copy.wait()
    tid = til_v[...]
    rid = own_v[...] * 256 + (tid >> 3)
    ry = ((rid >> 1) & 3) * 2 + ((rid >> 6) & 1)
    rz = rid >> 7
    dx = (((rid >> 3) & 3) - x) & 3
    block = jnp.where(dx == 2, 0, jnp.where(dx == 0, 3, (dx + 1) >> 1))
    first_step = (ry * swap + rz * core - (y * swap + z * core)) & 7
    second_step = (rz * swap + ry * core - (z * swap + y * core)) & 7
    spot = block * 128 + first_step * 16 + second_step * 2 + (rid & 1)
    spot = jnp.where(((rid >> 5) & 1) == core, spot, -1)
    idpad[...] = jnp.zeros((32, 256), jnp.int32)
    idpad[:, 0:192] = spot
    rowk[0:32, :] = idpad[:, 0:128]
    rowk[32:48, :] = jnp.where(
        lanes((16, 128)) < 64, idpad[0:16, 128:256], pltpu.roll(idpad[16:32, 128:256], 64, 1)
    )
    live = sublanes((32, 192)) + y_hi * 32 < jnp.broadcast_to(pc_v[...], (32, 192))
    shift_rows = jnp.where(live, tid & 7, SHIFTS).astype(F32)
    shift_rows = jnp.concatenate([shift_rows, jnp.full((96, 192), float(SHIFTS), F32)], axis=0)
    eye = (sublanes((192, 192)) == lanes((192, 192))).astype(F32).astype(BF16)
    shm_scr[...] = lax.dot_general(eye, shift_rows.astype(BF16), NT, preferred_element_type=F32)

    def roll_frames(source, half):
        def body(q, _):
            tile = source[:, pl.ds(pl.multiple_of(q * 128, 128), 128)].astype(F32)
            for s in range(SHIFTS):
                moved = pltpu.roll(tile, 17 * s, 1) if s else tile
                grolled[q, half * 128 + s * 16 : half * 128 + (s + 1) * 16, :] = moved.astype(BF16)
            return 0

        lax.fori_loop(0, 32, body, 0, unroll=4)

    def onehot(first, last):
        def body(kb, _):
            line = jnp.broadcast_to(rowk[pl.ds(kb, 1), :], (128, 128))
            for b in range(4):
                hit = line == sublanes((128, 128)) + b * 128
                ohs[b * 128 : (b + 1) * 128, pl.ds(pl.multiple_of(kb * 128, 128), 128)] = jnp.where(
                    hit, 1.0, 0.0
                ).astype(BF16)
            return 0

        lax.fori_loop(first, last, body, 0, unroll=2)

    roll_frames(cnt, 0)
    onehot(0, 16)

    for copy in p_copies:
        copy.wait_recv()
    score = (psend[...] + precv[0] + precv[1] + precv[2]) * (1.0 / math.sqrt(PIXELS))
    score_a, tail = score[0:16], score[16:24]
    off = -3.0e38
    score_b = jnp.concatenate(
        [jnp.where(lane8 < 64, tail, off), jnp.where(lane8 < 64, pltpu.roll(tail, 64, 1), off)], axis=0
    )
    top = jnp.maximum(
        jnp.max(score_a, axis=1, keepdims=True), jnp.max(score_b, axis=1, keepdims=True)
    )
    exp_a = jnp.exp(score_a - top)
    exp_b = jnp.exp(score_b - top)
    total = jnp.sum(exp_a, axis=1, keepdims=True) + jnp.sum(exp_b, axis=1, keepdims=True)
    ssend[0:8, :] = jnp.where(
        lane8 < 64,
        jnp.where(lane8 < 32, top[0:8], total[0:8]),
        jnp.where(lane8 < 96, top[8:16], total[8:16]),
    )
    ssend[8:24, :] = exp_a
    ssend[24:32, :] = jnp.where(lane8 < 64, exp_b[0:8], pltpu.roll(exp_b[8:16], 64, 1))
    s_copies = []
    for d in FAR4[:3]:
        for rel, cc in enumerate((core, swap)):
            slot = (d - 1) * 2 + rel
            s_copies.append(
                pltpu.make_async_remote_copy(
                    ssend.at[0:8], srecv.at[slot], s_send.at[slot], s_recv.at[slot],
                    device_id=place((x + d) % XN, y, z, cc),
                )
            )
    s_copies.append(
        pltpu.make_async_remote_copy(
            ssend, ppart, s_send.at[6], s_recv.at[6], device_id=place(x, y, z, swap)
        )
    )
    for copy in s_copies:
        copy.start()

    swap_frames.wait_recv()
    roll_frames(pcnt, 1)
    onehot(16, 48)

    for copy in s_copies:
        copy.wait_recv()

    def probabilities(packed, others):
        stats = packed[0:8, :]
        every = [stats, *others]
        most = functools.reduce(jnp.maximum, every)
        scale = pltpu.roll(jnp.exp(stats - most), 32, 1)
        whole = stats * scale
        for other in others:
            whole = whole + other * pltpu.roll(jnp.exp(other - most), 32, 1)
        factor = scale / whole
        low, high = factor[:, 32:33], factor[:, 96:97]
        prob_a = jnp.concatenate([packed[8:16, :] * low, packed[16:24, :] * high], axis=0)
        tail = packed[24:32, :]
        prob_b = jnp.concatenate([tail * low, pltpu.roll(tail, 64, 1) * high], axis=0)
        return prob_a.astype(BF16), prob_b.astype(BF16)

    own_a, own_b = probabilities(ssend, [srecv[0], srecv[2], srecv[4]])
    her_a, her_b = probabilities(ppart, [srecv[1], srecv[3], srecv[5]])
    prob_out[:, 0:128] = own_a
    prob_out[:, 128:192] = own_b[:, 0:64]

    stack = jnp.concatenate(
        [
            jnp.concatenate([own_a, own_b], axis=1)] * SHIFTS + [
            jnp.concatenate([her_a, her_b], axis=1)] * SHIFTS,
        axis=0,
    )
    eye = (sublanes((192, 256)) == lanes((192, 256))).astype(F32).astype(BF16)
    rep = lax.dot_general(eye, stack, NT, preferred_element_type=F32)
    rep_scr[...] = rep.astype(BF16)
    lane_shift = (lanes((192, 256)) % 128) // 16
    weights = jnp.dot(
        jnp.where(lane_shift == 0, rep, 0.0).astype(BF16), jnp.ones((256, 128), BF16), preferred_element_type=F32
    )
    upper = weights.astype(BF16).astype(F32)
    wsel_scr[...] = jnp.where(lanes((192, 128)) < 64, upper, weights - upper).astype(BF16)

    def patches(t4, _):
        columns = pltpu.roll(shm_scr[...], 128 - 4 * t4, 1)
        lane = ((lanes((192, 128)) % 128) // 16).astype(F32).astype(BF16)
        nil = jnp.zeros((192, 128), BF16)
        limit = jnp.full((192, 128), SHIFTS, BF16)
        for u in range(4):
            t = t4 * 4 + u
            for h in range(2):
                q = t + 16 * h
                shift = jnp.broadcast_to(columns[:, u + 16 * h : u + 16 * h + 1], (192, 128)).astype(BF16)
                same = shift == lane
                left = jnp.concatenate(
                    [jnp.where(same, rep_scr[:, 0:128], nil), jnp.where(same, rep_scr[:, 128:256], nil)], axis=1
                )
                moved = jnp.dot(left, grolled[q], preferred_element_type=F32).astype(BF16)
                weighed = jnp.where(shift < limit, wsel_scr[...], nil)
                both = jnp.concatenate([moved, weighed], axis=1)
                rhs[pl.ds(pl.multiple_of(q * 128, 128), 128), :] = both[0:128]
                rhs[pl.ds(pl.multiple_of(4096 + t * 128 + h * 64, 64), 64), :] = both[128:192]
        return 0

    lax.fori_loop(0, 4, patches, 0)

    diagonal = sublanes((128, 128)) == lanes((128, 128))
    x_copies = []
    for block, dx in enumerate(FAR4):
        total = jnp.dot(ohs[block * 128 : (block + 1) * 128, :], rhs[...], preferred_element_type=F32)
        halves = total[:, 128:256]
        weighed = jnp.where(diagonal, halves + pltpu.roll(halves, 64, 1), 0.0)
        line = jnp.broadcast_to(jnp.sum(weighed, axis=0, keepdims=True), (8, 128))
        for df in range(8):
            xs[block * 8 + df, 0:16, :] = total[df * 16 : (df + 1) * 16, 0:128]
            xs[block * 8 + df, 16:24, :] = pltpu.roll(line, 128 - 16 * df, 1) if df else line
        for df in (*FAR8, 0):
            if dx == 0 and df == 0:
                continue
            at = block * 8 + df
            slot = at if dx else at - 1
            copy = pltpu.make_async_remote_copy(
                xs.at[at, 0:17], xr.at[slot, 0:17], x_send.at[slot], x_recv.at[slot], device_id=along_first(dx, df)
            )
            copy.start()
            x_copies.append((slot, copy))
    brick = xs[24]
    for slot, copy in x_copies:
        copy.wait_recv()
        brick = brick + xr[slot]
    x_copies = [copy for _, copy in x_copies]

    sub8 = sublanes((8, 128))
    for k in range(8):
        tile = brick[8 * (k // 4) : 8 * (k // 4) + 8]
        tile = pltpu.roll(tile, 8 - 2 * (k % 4), 0) if k % 4 else tile
        line = jnp.broadcast_to(brick[16:17], (8, 128))
        line = pltpu.roll(line, 128 - 2 * k, 1) if k else line
        bsd[k] = jnp.where(sub8 < 2, tile, line)
    b_copies = [
        pltpu.make_async_remote_copy(
            bsd.at[d], br.at[d - 1], b_send.at[d - 1], b_recv.at[d - 1],
            device_id=place(x, (y + core * d) % YN, (z + swap * d) % ZN, core),
        )
        for d in FAR8
    ]
    for copy in b_copies:
        copy.start()
    last = bsd[0]
    for d, copy in zip(FAR8, b_copies):
        copy.wait_recv()
        last = last + br[d - 1]
    weight = jnp.sum(jnp.where(lanes((2, 128)) == sublanes((2, 128)), last[2:4], 0.0), axis=1, keepdims=True)
    merged_out[...] = (last[0:2] + PRIOR * old_v[...]) / (weight + PRIOR)

    swap_frames.wait_send()
    for copy in (*p_copies, *s_copies, *x_copies, *b_copies):
        copy.wait_send()


def shards(photon_counts, slices, owner_ids, tile_ids, patch_count, old_model):
    dma = pltpu.SemaphoreType.DMA
    return pl.pallas_call(
        kernel,
        out_shape=(jax.ShapeDtypeStruct((16, 192), BF16), jax.ShapeDtypeStruct((2, 128), F32)),
        in_specs=[pl.BlockSpec(memory_space=pl.ANY)] * 6,
        out_specs=(pl.BlockSpec(memory_space=pltpu.VMEM), pl.BlockSpec(memory_space=pltpu.VMEM)),
        scratch_shapes=[
            pltpu.VMEM((16, 4096), jnp.int32),
            pltpu.VMEM((16, 4096), jnp.int32),
            pltpu.VMEM((192, 4096), BF16),
            pltpu.VMEM((32, 192), jnp.int32),
            pltpu.VMEM((32, 192), jnp.int32),
            pltpu.VMEM((1, 192), jnp.int32),
            pltpu.VMEM((2, 128), F32),
            pltpu.VMEM((32, 256), jnp.int32),
            pltpu.VMEM((16, 256), F32),
            pltpu.VMEM((192, 128), F32),
            pltpu.VMEM((192, 256), BF16),
            pltpu.VMEM((192, 128), BF16),
            pltpu.VMEM((32, 256, 128), BF16),
            pltpu.VMEM((48, 128), jnp.int32),
            pltpu.VMEM((ROWS, KTOT), BF16),
            pltpu.VMEM((KTOT, 256), BF16),
            pltpu.VMEM((24, 128), F32),
            pltpu.VMEM((3, 24, 128), F32),
            pltpu.VMEM((32, 128), F32),
            pltpu.VMEM((6, 8, 128), F32),
            pltpu.VMEM((32, 128), F32),
            pltpu.VMEM((32, 24, 128), F32),
            pltpu.VMEM((31, 24, 128), F32),
            pltpu.VMEM((8, 8, 128), F32),
            pltpu.VMEM((7, 8, 128), F32),
            dma((9,)),
            dma((1,)), dma((1,)),
            dma((3,)), dma((3,)),
            dma((7,)), dma((7,)),
            dma((31,)), dma((31,)),
            dma((7,)), dma((7,)),
        ],
        compiler_params=pltpu.CompilerParams(
            collective_id=0, has_side_effects=True, vmem_limit_bytes=60 * 1024 * 1024
        ),
        cost_estimate=pl.CostEstimate(flops=2 * 10**9, bytes_accessed=2 * 10**6, transcendentals=10**6),
        name="em_step",
    )(photon_counts, slices, owner_ids.T, tile_ids.T, patch_count.reshape(1, -1), old_model)


def solution(mesh):
    placed = (
        P("frame", "pix"),
        P("orient", "pix"),
        P("orient", "pix"),
        P("orient", "pix"),
        P("orient"),
        P(("frame", "orient", "pix"), None),
    )
    return jax.shard_map(
        shards,
        mesh=mesh,
        in_specs=placed,
        out_specs=(P("frame", "orient"), P(("frame", "orient", "pix"), None)),
        check_vma=False,
    )
```

```python
import functools
import math

import jax
import jax.numpy as jnp
from jax import lax
from jax.experimental import pallas as pl
from jax.experimental.pallas import tpu as pltpu
from jax.sharding import PartitionSpec as P

XN, YN, ZN = 4, 8, 8
FAR8 = (4, 3, 5, 2, 6, 1, 7)
FAR4 = (2, 1, 3, 0)
PLACES = sorted(
    ((dx, df) for df in range(8) for dx in range(4)), key=lambda p: -min(p[0], 4 - p[0]) - min(p[1], 8 - p[1])
)
PIXELS = 16384
SHIFTS = 8
PRIOR = 512 * 128 / (4.0 * 1024)
ROWS = 512
KTOT = 192 * 32
F32 = jnp.float32
BF16 = jnp.bfloat16
NT = (((1,), (1,)), ((), ()))


def lanes(shape):
    return lax.broadcasted_iota(jnp.int32, shape, len(shape) - 1)


def sublanes(shape):
    return lax.broadcasted_iota(jnp.int32, shape, len(shape) - 2)


def kernel(
    counts_in, slices_in, owner_in, tile_in, count_in, old_in,
    prob_out, merged_out,
    cnt, pcnt, sl, own_v, til_v, pc_v, old_v,
    idpad, fit_scr, shm_scr, rep_scr, wsel_scr, col_scr, lhs, grolled, rowk, ohs, rhs,
    psend, precv, ssend, srecv, ppart,
    xs, xr, bsd, br,
    loc_sem, fr_send, fr_recv, p_send, p_recv, s_send, s_recv, x_send, x_recv, b_send, b_recv,
):
    fi = lax.axis_index("frame")
    x = lax.axis_index("orient")
    y_hi = lax.axis_index("pix")
    z = fi // 4
    y_lo = (fi // 2) % 2
    core = fi % 2
    y = y_hi * 2 + y_lo
    swap = 1 - core

    def place(xx, yy, zz, cc):
        return {"frame": zz * 4 + (yy % 2) * 2 + cc, "orient": xx, "pix": yy // 2}

    def along_first(dx, df):
        return place((x + dx) % XN, (y + swap * df) % YN, (z + core * df) % ZN, core)

    locals_ = [
        pltpu.make_async_copy(counts_in, cnt, loc_sem.at[0]),
        *[
            pltpu.make_async_copy(
                slices_in.at[:, c * 1024 : (c + 1) * 1024], sl.at[:, c * 1024 : (c + 1) * 1024], loc_sem.at[1 + c]
            )
            for c in range(4)
        ],
        pltpu.make_async_copy(owner_in, own_v, loc_sem.at[5]),
        pltpu.make_async_copy(tile_in, til_v, loc_sem.at[6]),
        pltpu.make_async_copy(count_in, pc_v, loc_sem.at[7]),
        pltpu.make_async_copy(old_in, old_v, loc_sem.at[8]),
    ]
    for copy in locals_:
        copy.start()

    barrier = pltpu.get_barrier_semaphore()
    for d in FAR8:
        pl.semaphore_signal(barrier, inc=1, device_id=place(x, (y + core * d) % YN, (z + swap * d) % ZN, core))
    for dx, df in PLACES[:31]:
        pl.semaphore_signal(barrier, inc=1, device_id=along_first(dx, df))
    for d in FAR4[:3]:
        pl.semaphore_signal(barrier, inc=1, device_id=place((x + d) % XN, y, z, swap))
    pl.semaphore_signal(barrier, inc=1, device_id=place(x, y, z, swap))

    locals_[0].wait()
    fit = jnp.zeros((16, 192), F32)
    mass = jnp.zeros((192, 128), F32)
    for c in range(16):
        if c % 4 == 0:
            locals_[1 + c // 4].wait()
        s32 = sl[:, c * 256 : (c + 1) * 256].astype(F32)
        mass = mass + (s32[:, :128] + s32[:, 128:])
        fr = cnt[:, c * 256 : (c + 1) * 256].astype(F32).astype(BF16)
        fit = fit + lax.dot_general(fr, jnp.log(s32).astype(BF16), NT, preferred_element_type=F32)
    fit = fit - lax.dot_general(
        jnp.ones((16, 128), F32), mass, NT, precision=lax.Precision.HIGHEST, preferred_element_type=F32
    )
    fit_scr[...] = jnp.zeros((16, 256), F32)
    fit_scr[:, 0:192] = fit
    lane8 = lanes((8, 128))
    psend[0:16, :] = fit_scr[:, 0:128]
    psend[16:24, :] = jnp.where(lane8 < 64, fit_scr[0:8, 128:256], pltpu.roll(fit_scr[8:16, 128:256], 64, 1))

    pl.semaphore_wait(barrier, 7 + 31 + 3 + 1)

    p_copies = [
        pltpu.make_async_remote_copy(
            psend, precv.at[d - 1], p_send.at[d - 1], p_recv.at[d - 1],
            device_id=place(x, (y + 2 * d) % YN, z, core),
        )
        for d in (2, 1, 3)
    ]
    for copy in p_copies:
        copy.start()
    swap_frames = pltpu.make_async_remote_copy(
        cnt, pcnt, fr_send.at[0], fr_recv.at[0], device_id=place(x, y, z, swap)
    )
    swap_frames.start()

    for copy in locals_[5:]:
        copy.wait()
    tid = til_v[...]
    rid = own_v[...] * 256 + (tid >> 3)
    ry = ((rid >> 1) & 3) * 2 + ((rid >> 6) & 1)
    rz = rid >> 7
    dx = (((rid >> 3) & 3) - x) & 3
    first_step = (ry * swap + rz * core - (y * swap + z * core)) & 7
    second_step = (rz * swap + ry * core - (z * swap + y * core)) & 7
    where_to = dx * 8 + first_step
    spot = jnp.full((32, 192), 31 * 16, jnp.int32)
    for at, (dx, df) in enumerate(PLACES[:31]):
        spot = jnp.where(where_to == dx * 8 + df, at * 16, spot)
    spot = spot + second_step * 2 + (rid & 1)
    spot = jnp.where(((rid >> 5) & 1) == core, spot, -1)
    idpad[...] = jnp.zeros((32, 256), jnp.int32)
    idpad[:, 0:192] = spot
    rowk[0:32, :] = idpad[:, 0:128]
    rowk[32:48, :] = jnp.where(
        lanes((16, 128)) < 64, idpad[0:16, 128:256], pltpu.roll(idpad[16:32, 128:256], 64, 1)
    )
    live = sublanes((32, 192)) + y_hi * 32 < jnp.broadcast_to(pc_v[...], (32, 192))
    shift_rows = jnp.where(live, tid & 7, SHIFTS).astype(F32)
    shift_rows = jnp.concatenate([shift_rows, jnp.full((96, 192), float(SHIFTS), F32)], axis=0)
    eye = (sublanes((192, 192)) == lanes((192, 192))).astype(F32).astype(BF16)
    shm_scr[...] = lax.dot_general(eye, shift_rows.astype(BF16), NT, preferred_element_type=F32)

    def roll_frames(source, half):
        def body(q, _):
            tile = source[:, pl.ds(pl.multiple_of(q * 128, 128), 128)].astype(F32)
            for s in range(SHIFTS):
                moved = pltpu.roll(tile, 17 * s, 1) if s else tile
                grolled[q, half * 128 + s * 16 : half * 128 + (s + 1) * 16, :] = moved.astype(BF16)
            return 0

        lax.fori_loop(0, 32, body, 0, unroll=4)

    def onehot(first, last):
        def body(kb, _):
            line = jnp.broadcast_to(rowk[pl.ds(kb, 1), :], (128, 128))
            for b in range(4):
                hit = line == sublanes((128, 128)) + b * 128
                ohs[b * 128 : (b + 1) * 128, pl.ds(pl.multiple_of(kb * 128, 128), 128)] = jnp.where(
                    hit, 1.0, 0.0
                ).astype(BF16)
            return 0

        lax.fori_loop(first, last, body, 0, unroll=2)

    roll_frames(cnt, 0)
    onehot(0, 48)
    swap_frames.wait_recv()
    roll_frames(pcnt, 1)

    for copy in p_copies:
        copy.wait_recv()
    score = (psend[...] + precv[0] + precv[1] + precv[2]) * (1.0 / math.sqrt(PIXELS))
    score_a, tail = score[0:16], score[16:24]
    off = -3.0e38
    score_b = jnp.concatenate(
        [jnp.where(lane8 < 64, tail, off), jnp.where(lane8 < 64, pltpu.roll(tail, 64, 1), off)], axis=0
    )
    top = jnp.maximum(
        jnp.max(score_a, axis=1, keepdims=True), jnp.max(score_b, axis=1, keepdims=True)
    )
    exp_a = jnp.exp(score_a - top)
    exp_b = jnp.exp(score_b - top)
    total = jnp.sum(exp_a, axis=1, keepdims=True) + jnp.sum(exp_b, axis=1, keepdims=True)
    ssend[0:8, :] = jnp.where(
        lane8 < 64,
        jnp.where(lane8 < 32, top[0:8], total[0:8]),
        jnp.where(lane8 < 96, top[8:16], total[8:16]),
    )
    ssend[8:24, :] = exp_a
    ssend[24:32, :] = jnp.where(lane8 < 64, exp_b[0:8], pltpu.roll(exp_b[8:16], 64, 1))
    s_copies = []
    for d in FAR4[:3]:
        for rel, cc in enumerate((core, swap)):
            slot = (d - 1) * 2 + rel
            s_copies.append(
                pltpu.make_async_remote_copy(
                    ssend.at[0:8], srecv.at[slot], s_send.at[slot], s_recv.at[slot],
                    device_id=place((x + d) % XN, y, z, cc),
                )
            )
    s_copies.append(
        pltpu.make_async_remote_copy(
            ssend, ppart, s_send.at[6], s_recv.at[6], device_id=place(x, y, z, swap)
        )
    )
    for copy in s_copies:
        copy.start()

    s_copies[-1].wait_recv()

    def spread(packed):
        tail = packed[24:32, :]
        tail = jnp.concatenate([tail, pltpu.roll(tail, 64, 1)], axis=0)
        both = jnp.concatenate([packed[8:24, :], tail], axis=1).astype(BF16)
        return [both] * SHIFTS

    eye = (sublanes((192, 256)) == lanes((192, 256))).astype(F32).astype(BF16)
    stack = jnp.concatenate(spread(ssend) + spread(ppart), axis=0)
    rep_scr[...] = lax.dot_general(eye, stack, NT, preferred_element_type=F32).astype(BF16)

    def selections(t4, _):
        columns = pltpu.roll(shm_scr[...], 128 - 4 * t4, 1)
        lane = ((lanes((192, 128)) % 128) // 16).astype(F32).astype(BF16)
        nil = jnp.zeros((192, 128), BF16)
        one = jnp.ones((192, 128), BF16)
        limit = jnp.full((192, 128), SHIFTS, BF16)
        for u in range(4):
            for h in range(2):
                q = t4 * 4 + u + 16 * h
                shift = jnp.broadcast_to(columns[:, u + 16 * h : u + 16 * h + 1], (192, 128)).astype(BF16)
                same = shift == lane
                lhs[q, :, 0:128] = jnp.where(same, rep_scr[:, 0:128], nil)
                lhs[q, :, 128:256] = jnp.where(same, rep_scr[:, 128:256], nil)
                lhs[q, :, 256:384] = jnp.where(shift < limit, one, nil)
        return 0

    lax.fori_loop(0, 4, selections, 0)

    for copy in s_copies[:-1]:
        copy.wait_recv()

    def factors(packed, others):
        stats = packed[0:8, :]
        every = [stats, *others]
        most = functools.reduce(jnp.maximum, every)
        scale = pltpu.roll(jnp.exp(stats - most), 32, 1)
        whole = stats * scale
        for other in others:
            whole = whole + other * pltpu.roll(jnp.exp(other - most), 32, 1)
        factor = scale / whole
        return jnp.broadcast_to(factor[:, 32:33], (8, 128)), jnp.broadcast_to(factor[:, 96:97], (8, 128))

    low, high = factors(ssend, [srecv[0], srecv[2], srecv[4]])
    her_low, her_high = factors(ppart, [srecv[1], srecv[3], srecv[5]])
    column = jnp.concatenate([low, high] * SHIFTS + [her_low, her_high] * SHIFTS, axis=0)
    col_scr[...] = column
    upper = column.astype(BF16).astype(F32)
    parts = jnp.where(lanes((256, 128)) < 64, upper, column - upper).astype(BF16)
    unshifted = jnp.where((lanes((192, 256)) % 128) // 16 == 0, rep_scr[...].astype(F32), 0.0).astype(BF16)
    weights = jnp.dot(unshifted, parts, preferred_element_type=F32)
    weights = weights + pltpu.roll(weights, 64, 1)
    upper = weights.astype(BF16).astype(F32)
    wsel_scr[...] = jnp.where(lanes((192, 128)) < 64, upper, weights - upper).astype(BF16)

    def patches(t4, _):
        for u in range(4):
            t = t4 * 4 + u
            for h in range(2):
                q = t + 16 * h
                scaled = (grolled[q].astype(F32) * col_scr[...]).astype(BF16)
                moved = jnp.dot(lhs[q, :, 0:256], scaled, preferred_element_type=F32).astype(BF16)
                both = jnp.concatenate([moved, lhs[q, :, 256:384] * wsel_scr[...]], axis=1)
                rhs[pl.ds(pl.multiple_of(q * 128, 128), 128), :] = both[0:128]
                rhs[pl.ds(pl.multiple_of(4096 + t * 128 + h * 64, 64), 64), :] = both[128:192]
        return 0

    lax.fori_loop(0, 4, patches, 0)

    diagonal = sublanes((128, 128)) == lanes((128, 128))
    x_copies = []
    for block in range(4):
        total = jnp.dot(ohs[block * 128 : (block + 1) * 128, :], rhs[...], preferred_element_type=F32)
        halves = total[:, 128:256]
        weighed = jnp.where(diagonal, halves + pltpu.roll(halves, 64, 1), 0.0)
        line = jnp.broadcast_to(jnp.sum(weighed, axis=0, keepdims=True), (8, 128))
        for k in range(8):
            xs[block * 8 + k, 0:16, :] = total[k * 16 : (k + 1) * 16, 0:128]
            xs[block * 8 + k, 16:24, :] = pltpu.roll(line, 128 - 16 * k, 1) if k else line
        for at in range(block * 8, min(block * 8 + 8, 31)):
            copy = pltpu.make_async_remote_copy(
                xs.at[at, 0:17], xr.at[at, 0:17], x_send.at[at], x_recv.at[at], device_id=along_first(*PLACES[at])
            )
            copy.start()
            x_copies.append(copy)
    tail = ssend[24:32, :]
    prob_out[:, 0:128] = jnp.concatenate([ssend[8:16, :] * low, ssend[16:24, :] * high], axis=0).astype(BF16)
    prob_out[:, 128:192] = jnp.concatenate([tail * low, pltpu.roll(tail, 64, 1) * high], axis=0)[:, 0:64].astype(BF16)
    brick = xs[31]
    for at, copy in enumerate(x_copies):
        copy.wait_recv()
        brick = brick + xr[at]

    sub8 = sublanes((8, 128))
    for k in range(8):
        tile = brick[8 * (k // 4) : 8 * (k // 4) + 8]
        tile = pltpu.roll(tile, 8 - 2 * (k % 4), 0) if k % 4 else tile
        line = jnp.broadcast_to(brick[16:17], (8, 128))
        line = pltpu.roll(line, 128 - 2 * k, 1) if k else line
        bsd[k] = jnp.where(sub8 < 2, tile, line)
    b_copies = [
        pltpu.make_async_remote_copy(
            bsd.at[d], br.at[d - 1], b_send.at[d - 1], b_recv.at[d - 1],
            device_id=place(x, (y + core * d) % YN, (z + swap * d) % ZN, core),
        )
        for d in FAR8
    ]
    for copy in b_copies:
        copy.start()
    last = bsd[0]
    for d, copy in zip(FAR8, b_copies):
        copy.wait_recv()
        last = last + br[d - 1]
    weight = jnp.sum(jnp.where(lanes((2, 128)) == sublanes((2, 128)), last[2:4], 0.0), axis=1, keepdims=True)
    merged_out[...] = (last[0:2] + PRIOR * old_v[...]) / (weight + PRIOR)

    swap_frames.wait_send()
    for copy in (*p_copies, *s_copies, *x_copies, *b_copies):
        copy.wait_send()


def hand_on(prob_in, merged_in, prob_out, merged_out, sem):
    copies = [pltpu.make_async_copy(prob_in, prob_out, sem.at[0]), pltpu.make_async_copy(merged_in, merged_out, sem.at[1])]
    for copy in copies:
        copy.start()
    for copy in copies:
        copy.wait()


def shards(photon_counts, slices, owner_ids, tile_ids, patch_count, old_model):
    dma = pltpu.SemaphoreType.DMA
    prob, merged = pl.pallas_call(
        kernel,
        out_shape=(jax.ShapeDtypeStruct((16, 192), BF16), jax.ShapeDtypeStruct((2, 128), F32)),
        in_specs=[pl.BlockSpec(memory_space=pl.ANY)] * 6,
        out_specs=(pl.BlockSpec(memory_space=pltpu.VMEM), pl.BlockSpec(memory_space=pltpu.VMEM)),
        scratch_shapes=[
            pltpu.VMEM((16, 4096), jnp.int32),
            pltpu.VMEM((16, 4096), jnp.int32),
            pltpu.VMEM((192, 4096), BF16),
            pltpu.VMEM((32, 192), jnp.int32),
            pltpu.VMEM((32, 192), jnp.int32),
            pltpu.VMEM((1, 192), jnp.int32),
            pltpu.VMEM((2, 128), F32),
            pltpu.VMEM((32, 256), jnp.int32),
            pltpu.VMEM((16, 256), F32),
            pltpu.VMEM((192, 128), F32),
            pltpu.VMEM((192, 256), BF16),
            pltpu.VMEM((192, 128), BF16),
            pltpu.VMEM((256, 128), F32),
            pltpu.VMEM((32, 192, 384), BF16),
            pltpu.VMEM((32, 256, 128), BF16),
            pltpu.VMEM((48, 128), jnp.int32),
            pltpu.VMEM((ROWS, KTOT), BF16),
            pltpu.VMEM((KTOT, 256), BF16),
            pltpu.VMEM((24, 128), F32),
            pltpu.VMEM((3, 24, 128), F32),
            pltpu.VMEM((32, 128), F32),
            pltpu.VMEM((6, 8, 128), F32),
            pltpu.VMEM((32, 128), F32),
            pltpu.VMEM((32, 24, 128), F32),
            pltpu.VMEM((31, 24, 128), F32),
            pltpu.VMEM((8, 8, 128), F32),
            pltpu.VMEM((7, 8, 128), F32),
            dma((9,)),
            dma((1,)), dma((1,)),
            dma((3,)), dma((3,)),
            dma((7,)), dma((7,)),
            dma((31,)), dma((31,)),
            dma((7,)), dma((7,)),
        ],
        compiler_params=pltpu.CompilerParams(
            collective_id=0, has_side_effects=True, vmem_limit_bytes=60 * 1024 * 1024
        ),
        cost_estimate=pl.CostEstimate(flops=2 * 10**9, bytes_accessed=2 * 10**6, transcendentals=10**6),
        name="em_step",
    )(photon_counts, slices, owner_ids.T, tile_ids.T, patch_count.reshape(1, -1), old_model)
    anywhere = pl.BlockSpec(memory_space=pl.ANY)
    return pl.pallas_call(
        hand_on,
        out_shape=(jax.ShapeDtypeStruct((16, 192), BF16), jax.ShapeDtypeStruct((2, 128), F32)),
        in_specs=[anywhere, anywhere],
        out_specs=(anywhere, anywhere),
        scratch_shapes=[dma((2,))],
        compiler_params=pltpu.CompilerParams(vmem_limit_bytes=60 * 1024 * 1024),
        name="hand_on",
    )(prob, merged)


def solution(mesh):
    placed = (
        P("frame", "pix"),
        P("orient", "pix"),
        P("orient", "pix"),
        P("orient", "pix"),
        P("orient"),
        P(("frame", "orient", "pix"), None),
    )
    return jax.shard_map(
        shards,
        mesh=mesh,
        in_specs=placed,
        out_specs=(P("frame", "orient"), P(("frame", "orient", "pix"), None)),
        check_vma=False,
    )
```

```python
import functools
import math

import jax
import jax.numpy as jnp
from jax import lax
from jax.experimental import pallas as pl
from jax.experimental.pallas import tpu as pltpu
from jax.sharding import PartitionSpec as P

XN, YN, ZN = 4, 8, 8
FAR8 = (4, 3, 5, 2, 6, 1, 7)
FAR4 = (2, 1, 3, 0)
PLACES = sorted(
    ((dx, df) for df in range(8) for dx in range(4)), key=lambda p: -min(p[0], 4 - p[0]) - min(p[1], 8 - p[1])
)
PIXELS = 16384
SHIFTS = 8
PRIOR = 512 * 128 / (4.0 * 1024)
ROWS = 512
KTOT = 192 * 32
F32 = jnp.float32
BF16 = jnp.bfloat16
NT = (((1,), (1,)), ((), ()))


def lanes(shape):
    return lax.broadcasted_iota(jnp.int32, shape, len(shape) - 1)


def sublanes(shape):
    return lax.broadcasted_iota(jnp.int32, shape, len(shape) - 2)


def kernel(
    counts_in, slices_in, owner_in, tile_in, count_in, old_in,
    prob_out, merged_out,
    cnt, pcnt, sl, own_v, til_v, pc_v, old_v,
    idpad, fit_scr, shm_scr, rep_scr, wsel_scr, col_scr, lhs, grolled, rowk, ohs, rhs,
    psend, precv, ssend, srecv, ppart,
    xs, xr, bsd, br,
    loc_sem, fr_send, fr_recv, p_send, p_recv, s_send, s_recv, x_send, x_recv, b_send, b_recv,
):
    fi = lax.axis_index("frame")
    x = lax.axis_index("orient")
    y_hi = lax.axis_index("pix")
    z = fi // 4
    y_lo = (fi // 2) % 2
    core = fi % 2
    y = y_hi * 2 + y_lo
    swap = 1 - core

    def place(xx, yy, zz, cc):
        return {"frame": zz * 4 + (yy % 2) * 2 + cc, "orient": xx, "pix": yy // 2}

    def along_first(dx, df):
        return place((x + dx) % XN, (y + swap * df) % YN, (z + core * df) % ZN, core)

    locals_ = [
        pltpu.make_async_copy(counts_in, cnt, loc_sem.at[0]),
        *[
            pltpu.make_async_copy(
                slices_in.at[:, c * 1024 : (c + 1) * 1024], sl.at[:, c * 1024 : (c + 1) * 1024], loc_sem.at[1 + c]
            )
            for c in range(4)
        ],
        pltpu.make_async_copy(owner_in, own_v, loc_sem.at[5]),
        pltpu.make_async_copy(tile_in, til_v, loc_sem.at[6]),
        pltpu.make_async_copy(count_in, pc_v, loc_sem.at[7]),
        pltpu.make_async_copy(old_in, old_v, loc_sem.at[8]),
    ]
    for copy in locals_:
        copy.start()

    barrier = pltpu.get_barrier_semaphore()
    for d in FAR8:
        pl.semaphore_signal(barrier, inc=1, device_id=place(x, (y + core * d) % YN, (z + swap * d) % ZN, core))
    for dx, df in PLACES[:31]:
        pl.semaphore_signal(barrier, inc=1, device_id=along_first(dx, df))
    for d in FAR4[:3]:
        pl.semaphore_signal(barrier, inc=1, device_id=place((x + d) % XN, y, z, swap))
    pl.semaphore_signal(barrier, inc=1, device_id=place(x, y, z, swap))

    locals_[0].wait()
    fit = jnp.zeros((16, 192), F32)
    mass = jnp.zeros((192, 128), F32)
    for c in range(16):
        if c % 4 == 0:
            locals_[1 + c // 4].wait()
        s32 = sl[:, c * 256 : (c + 1) * 256].astype(F32)
        mass = mass + (s32[:, :128] + s32[:, 128:])
        fr = cnt[:, c * 256 : (c + 1) * 256].astype(F32).astype(BF16)
        fit = fit + lax.dot_general(fr, jnp.log(s32).astype(BF16), NT, preferred_element_type=F32)
    fit = fit - lax.dot_general(
        jnp.ones((16, 128), F32), mass, NT, precision=lax.Precision.HIGHEST, preferred_element_type=F32
    )
    fit_scr[...] = jnp.zeros((16, 256), F32)
    fit_scr[:, 0:192] = fit
    lane8 = lanes((8, 128))
    psend[0:16, :] = fit_scr[:, 0:128]
    psend[16:24, :] = jnp.where(lane8 < 64, fit_scr[0:8, 128:256], pltpu.roll(fit_scr[8:16, 128:256], 64, 1))

    pl.semaphore_wait(barrier, 7 + 31 + 3 + 1)

    p_copies = [
        pltpu.make_async_remote_copy(
            psend, precv.at[d - 1], p_send.at[d - 1], p_recv.at[d - 1],
            device_id=place(x, (y + 2 * d) % YN, z, core),
        )
        for d in (2, 1, 3)
    ]
    for copy in p_copies:
        copy.start()
    swap_frames = pltpu.make_async_remote_copy(
        cnt, pcnt, fr_send.at[0], fr_recv.at[0], device_id=place(x, y, z, swap)
    )
    swap_frames.start()

    for copy in locals_[5:]:
        copy.wait()
    tid = til_v[...]
    rid = own_v[...] * 256 + (tid >> 3)
    ry = ((rid >> 1) & 3) * 2 + ((rid >> 6) & 1)
    rz = rid >> 7
    dx = (((rid >> 3) & 3) - x) & 3
    first_step = (ry * swap + rz * core - (y * swap + z * core)) & 7
    second_step = (rz * swap + ry * core - (z * swap + y * core)) & 7
    where_to = dx * 8 + first_step
    spot = jnp.full((32, 192), 31 * 16, jnp.int32)
    for at, (dx, df) in enumerate(PLACES[:31]):
        spot = jnp.where(where_to == dx * 8 + df, at * 16, spot)
    spot = spot + second_step * 2 + (rid & 1)
    spot = jnp.where(((rid >> 5) & 1) == core, spot, -1)
    idpad[...] = jnp.zeros((32, 256), jnp.int32)
    idpad[:, 0:192] = spot
    rowk[0:32, :] = idpad[:, 0:128]
    rowk[32:48, :] = jnp.where(
        lanes((16, 128)) < 64, idpad[0:16, 128:256], pltpu.roll(idpad[16:32, 128:256], 64, 1)
    )
    live = sublanes((32, 192)) + y_hi * 32 < jnp.broadcast_to(pc_v[...], (32, 192))
    shift_rows = jnp.where(live, tid & 7, SHIFTS).astype(F32)
    shift_rows = jnp.concatenate([shift_rows, jnp.full((96, 192), float(SHIFTS), F32)], axis=0)
    eye = (sublanes((192, 192)) == lanes((192, 192))).astype(F32).astype(BF16)
    shm_scr[...] = lax.dot_general(eye, shift_rows.astype(BF16), NT, preferred_element_type=F32)

    def roll_frames(source, half):
        def body(q, _):
            tile = source[:, pl.ds(pl.multiple_of(q * 128, 128), 128)].astype(F32)
            for s in range(SHIFTS):
                moved = pltpu.roll(tile, 17 * s, 1) if s else tile
                grolled[q, half * 128 + s * 16 : half * 128 + (s + 1) * 16, :] = moved.astype(BF16)
            return 0

        lax.fori_loop(0, 32, body, 0, unroll=4)

    def onehot(first, last):
        def body(kb, _):
            line = jnp.broadcast_to(rowk[pl.ds(kb, 1), :], (128, 128))
            for b in range(4):
                hit = line == sublanes((128, 128)) + b * 128
                ohs[b * 128 : (b + 1) * 128, pl.ds(pl.multiple_of(kb * 128, 128), 128)] = jnp.where(
                    hit, 1.0, 0.0
                ).astype(BF16)
            return 0

        lax.fori_loop(first, last, body, 0, unroll=2)

    roll_frames(cnt, 0)
    onehot(0, 48)
    swap_frames.wait_recv()
    roll_frames(pcnt, 1)

    for copy in p_copies:
        copy.wait_recv()
    score = (psend[...] + precv[0] + precv[1] + precv[2]) * (1.0 / math.sqrt(PIXELS))
    score_a, tail = score[0:16], score[16:24]
    off = -3.0e38
    score_b = jnp.concatenate(
        [jnp.where(lane8 < 64, tail, off), jnp.where(lane8 < 64, pltpu.roll(tail, 64, 1), off)], axis=0
    )
    top = jnp.maximum(
        jnp.max(score_a, axis=1, keepdims=True), jnp.max(score_b, axis=1, keepdims=True)
    )
    exp_a = jnp.exp(score_a - top)
    exp_b = jnp.exp(score_b - top)
    total = jnp.sum(exp_a, axis=1, keepdims=True) + jnp.sum(exp_b, axis=1, keepdims=True)
    ssend[0:8, :] = jnp.where(
        lane8 < 64,
        jnp.where(lane8 < 32, top[0:8], total[0:8]),
        jnp.where(lane8 < 96, top[8:16], total[8:16]),
    )
    ssend[8:24, :] = exp_a
    ssend[24:32, :] = jnp.where(lane8 < 64, exp_b[0:8], pltpu.roll(exp_b[8:16], 64, 1))
    s_copies = []
    for d in FAR4[:3]:
        for rel, cc in enumerate((core, swap)):
            slot = (d - 1) * 2 + rel
            s_copies.append(
                pltpu.make_async_remote_copy(
                    ssend.at[0:8], srecv.at[slot], s_send.at[slot], s_recv.at[slot],
                    device_id=place((x + d) % XN, y, z, cc),
                )
            )
    s_copies.append(
        pltpu.make_async_remote_copy(
            ssend, ppart, s_send.at[6], s_recv.at[6], device_id=place(x, y, z, swap)
        )
    )
    for copy in s_copies:
        copy.start()

    s_copies[-1].wait_recv()

    def spread(packed):
        tail = packed[24:32, :]
        tail = jnp.concatenate([tail, pltpu.roll(tail, 64, 1)], axis=0)
        both = jnp.concatenate([packed[8:24, :], tail], axis=1).astype(BF16)
        return [both] * SHIFTS

    eye = (sublanes((192, 256)) == lanes((192, 256))).astype(F32).astype(BF16)
    stack = jnp.concatenate(spread(ssend) + spread(ppart), axis=0)
    rep_scr[...] = lax.dot_general(eye, stack, NT, preferred_element_type=F32).astype(BF16)

    def selections(t4, _):
        columns = pltpu.roll(shm_scr[...], 128 - 4 * t4, 1)
        lane = ((lanes((192, 128)) % 128) // 16).astype(F32).astype(BF16)
        nil = jnp.zeros((192, 128), BF16)
        one = jnp.ones((192, 128), BF16)
        limit = jnp.full((192, 128), SHIFTS, BF16)
        for u in range(4):
            for h in range(2):
                q = t4 * 4 + u + 16 * h
                shift = jnp.broadcast_to(columns[:, u + 16 * h : u + 16 * h + 1], (192, 128)).astype(BF16)
                same = shift == lane
                lhs[q, :, 0:128] = jnp.where(same, rep_scr[:, 0:128], nil)
                lhs[q, :, 128:256] = jnp.where(same, rep_scr[:, 128:256], nil)
                lhs[q, :, 256:384] = jnp.where(shift < limit, one, nil)
        return 0

    lax.fori_loop(0, 4, selections, 0)

    for copy in s_copies[:-1]:
        copy.wait_recv()

    def factors(packed, others):
        stats = packed[0:8, :]
        every = [stats, *others]
        most = functools.reduce(jnp.maximum, every)
        scale = pltpu.roll(jnp.exp(stats - most), 32, 1)
        whole = stats * scale
        for other in others:
            whole = whole + other * pltpu.roll(jnp.exp(other - most), 32, 1)
        factor = scale / whole
        return jnp.broadcast_to(factor[:, 32:33], (8, 128)), jnp.broadcast_to(factor[:, 96:97], (8, 128))

    low, high = factors(ssend, [srecv[0], srecv[2], srecv[4]])
    her_low, her_high = factors(ppart, [srecv[1], srecv[3], srecv[5]])
    column = jnp.concatenate([low, high] * SHIFTS + [her_low, her_high] * SHIFTS, axis=0)
    col_scr[...] = column
    upper = column.astype(BF16).astype(F32)
    parts = jnp.where(lanes((256, 128)) < 64, upper, column - upper).astype(BF16)
    unshifted = jnp.where((lanes((192, 256)) % 128) // 16 == 0, rep_scr[...].astype(F32), 0.0).astype(BF16)
    weights = jnp.dot(unshifted, parts, preferred_element_type=F32)
    weights = weights + pltpu.roll(weights, 64, 1)
    upper = weights.astype(BF16).astype(F32)
    wsel_scr[...] = jnp.where(lanes((192, 128)) < 64, upper, weights - upper).astype(BF16)

    def patches(t4, _):
        for u in range(4):
            t = t4 * 4 + u
            for h in range(2):
                q = t + 16 * h
                scaled = (grolled[q].astype(F32) * col_scr[...]).astype(BF16)
                moved = jnp.dot(lhs[q, :, 0:256], scaled, preferred_element_type=F32).astype(BF16)
                both = jnp.concatenate([moved, lhs[q, :, 256:384] * wsel_scr[...]], axis=1)
                rhs[pl.ds(pl.multiple_of(q * 128, 128), 128), :] = both[0:128]
                rhs[pl.ds(pl.multiple_of(4096 + t * 128 + h * 64, 64), 64), :] = both[128:192]
        return 0

    lax.fori_loop(0, 4, patches, 0)

    diagonal = sublanes((128, 128)) == lanes((128, 128))
    x_copies = []
    for block in range(4):
        total = jnp.dot(ohs[block * 128 : (block + 1) * 128, :], rhs[...], preferred_element_type=F32)
        halves = total[:, 128:256]
        weighed = jnp.where(diagonal, halves + pltpu.roll(halves, 64, 1), 0.0)
        line = jnp.broadcast_to(jnp.sum(weighed, axis=0, keepdims=True), (8, 128))
        for k in range(8):
            xs[block * 8 + k, 0:16, :] = total[k * 16 : (k + 1) * 16, 0:128]
            xs[block * 8 + k, 16:24, :] = pltpu.roll(line, 128 - 16 * k, 1) if k else line
        for at in range(block * 8, min(block * 8 + 8, 31)):
            copy = pltpu.make_async_remote_copy(
                xs.at[at, 0:17], xr.at[at, 0:17], x_send.at[at], x_recv.at[at], device_id=along_first(*PLACES[at])
            )
            copy.start()
            x_copies.append(copy)
    tail = ssend[24:32, :]
    prob_out[:, 0:128] = jnp.concatenate([ssend[8:16, :] * low, ssend[16:24, :] * high], axis=0).astype(BF16)
    prob_out[:, 128:192] = jnp.concatenate([tail * low, pltpu.roll(tail, 64, 1) * high], axis=0)[:, 0:64].astype(BF16)
    brick = xs[31]
    for at, copy in enumerate(x_copies):
        copy.wait_recv()
        brick = brick + xr[at]

    sub8 = sublanes((8, 128))
    for k in range(8):
        tile = brick[8 * (k // 4) : 8 * (k // 4) + 8]
        tile = pltpu.roll(tile, 8 - 2 * (k % 4), 0) if k % 4 else tile
        line = jnp.broadcast_to(brick[16:17], (8, 128))
        line = pltpu.roll(line, 128 - 2 * k, 1) if k else line
        bsd[k] = jnp.where(sub8 < 2, tile, line)
    b_copies = [
        pltpu.make_async_remote_copy(
            bsd.at[d, 0:4], br.at[d - 1, 0:4], b_send.at[d - 1], b_recv.at[d - 1],
            device_id=place(x, (y + core * d) % YN, (z + swap * d) % ZN, core),
        )
        for d in FAR8
    ]
    for copy in b_copies:
        copy.start()
    last = bsd[0]
    for d, copy in zip(FAR8, b_copies):
        copy.wait_recv()
        last = last + br[d - 1]
    weight = jnp.sum(jnp.where(lanes((2, 128)) == sublanes((2, 128)), last[2:4], 0.0), axis=1, keepdims=True)
    merged_out[...] = (last[0:2] + PRIOR * old_v[...]) / (weight + PRIOR)

    swap_frames.wait_send()
    for copy in (*p_copies, *s_copies, *x_copies, *b_copies):
        copy.wait_send()


def hand_on(prob_in, merged_in, prob_out, merged_out):
    prob_out[...] = prob_in[...]
    merged_out[...] = merged_in[...]


def shards(photon_counts, slices, owner_ids, tile_ids, patch_count, old_model):
    dma = pltpu.SemaphoreType.DMA
    prob, merged = pl.pallas_call(
        kernel,
        out_shape=(jax.ShapeDtypeStruct((16, 192), BF16), jax.ShapeDtypeStruct((2, 128), F32)),
        in_specs=[pl.BlockSpec(memory_space=pl.ANY)] * 6,
        out_specs=(pl.BlockSpec(memory_space=pltpu.VMEM), pl.BlockSpec(memory_space=pltpu.VMEM)),
        scratch_shapes=[
            pltpu.VMEM((16, 4096), jnp.int32),
            pltpu.VMEM((16, 4096), jnp.int32),
            pltpu.VMEM((192, 4096), BF16),
            pltpu.VMEM((32, 192), jnp.int32),
            pltpu.VMEM((32, 192), jnp.int32),
            pltpu.VMEM((1, 192), jnp.int32),
            pltpu.VMEM((2, 128), F32),
            pltpu.VMEM((32, 256), jnp.int32),
            pltpu.VMEM((16, 256), F32),
            pltpu.VMEM((192, 128), F32),
            pltpu.VMEM((192, 256), BF16),
            pltpu.VMEM((192, 128), BF16),
            pltpu.VMEM((256, 128), F32),
            pltpu.VMEM((32, 192, 384), BF16),
            pltpu.VMEM((32, 256, 128), BF16),
            pltpu.VMEM((48, 128), jnp.int32),
            pltpu.VMEM((ROWS, KTOT), BF16),
            pltpu.VMEM((KTOT, 256), BF16),
            pltpu.VMEM((24, 128), F32),
            pltpu.VMEM((3, 24, 128), F32),
            pltpu.VMEM((32, 128), F32),
            pltpu.VMEM((6, 8, 128), F32),
            pltpu.VMEM((32, 128), F32),
            pltpu.VMEM((32, 24, 128), F32),
            pltpu.VMEM((31, 24, 128), F32),
            pltpu.VMEM((8, 8, 128), F32),
            pltpu.VMEM((7, 8, 128), F32),
            dma((9,)),
            dma((1,)), dma((1,)),
            dma((3,)), dma((3,)),
            dma((7,)), dma((7,)),
            dma((31,)), dma((31,)),
            dma((7,)), dma((7,)),
        ],
        compiler_params=pltpu.CompilerParams(
            collective_id=0, has_side_effects=True, vmem_limit_bytes=60 * 1024 * 1024
        ),
        cost_estimate=pl.CostEstimate(flops=2 * 10**9, bytes_accessed=2 * 10**6, transcendentals=10**6),
        name="em_step",
    )(photon_counts, slices, owner_ids.T, tile_ids.T, patch_count.reshape(1, -1), old_model)
    vmem = pl.BlockSpec(memory_space=pltpu.VMEM)
    return pl.pallas_call(
        hand_on,
        out_shape=(jax.ShapeDtypeStruct((16, 192), BF16), jax.ShapeDtypeStruct((2, 128), F32)),
        in_specs=[vmem, vmem],
        out_specs=(vmem, vmem),
        compiler_params=pltpu.CompilerParams(vmem_limit_bytes=60 * 1024 * 1024),
        name="hand_on",
    )(prob, merged)


def solution(mesh):
    placed = (
        P("frame", "pix"),
        P("orient", "pix"),
        P("orient", "pix"),
        P("orient", "pix"),
        P("orient"),
        P(("frame", "orient", "pix"), None),
    )
    return jax.shard_map(
        shards,
        mesh=mesh,
        in_specs=placed,
        out_specs=(P("frame", "orient"), P(("frame", "orient", "pix"), None)),
        check_vma=False,
    )
```

```python
import functools
import math

import jax
import jax.numpy as jnp
from jax import lax
from jax.experimental import pallas as pl
from jax.experimental.pallas import tpu as pltpu
from jax.sharding import PartitionSpec as P

XN, YN, ZN = 4, 8, 8
FAR8 = (4, 3, 5, 2, 6, 1, 7)
FAR4 = (2, 1, 3, 0)
PLACES = sorted(
    ((dx, df) for df in range(8) for dx in range(4)), key=lambda p: -min(p[0], 4 - p[0]) - min(p[1], 8 - p[1])
)
PIXELS = 16384
SHIFTS = 8
PRIOR = 512 * 128 / (4.0 * 1024)
ROWS = 512
KTOT = 192 * 32
F32 = jnp.float32
BF16 = jnp.bfloat16
NT = (((1,), (1,)), ((), ()))


def lanes(shape):
    return lax.broadcasted_iota(jnp.int32, shape, len(shape) - 1)


def sublanes(shape):
    return lax.broadcasted_iota(jnp.int32, shape, len(shape) - 2)


def kernel(
    counts_in, slices_in, owner_in, tile_in, count_in, old_in,
    prob_out, merged_out,
    cnt, pcnt, sl, own_v, til_v, pc_v, old_v,
    idpad, fit_scr, shm_scr, rep_scr, wsel_scr, col_scr, lhs, grolled, rowk, ohs, rhs,
    psend, precv, ssend, srecv, ppart,
    xs, xr, bsd, br,
    loc_sem, fr_send, fr_recv, p_send, p_recv, s_send, s_recv, x_send, x_recv, b_send, b_recv,
):
    fi = lax.axis_index("frame")
    x = lax.axis_index("orient")
    y_hi = lax.axis_index("pix")
    z = fi // 4
    y_lo = (fi // 2) % 2
    core = fi % 2
    y = y_hi * 2 + y_lo
    swap = 1 - core

    def place(xx, yy, zz, cc):
        return {"frame": zz * 4 + (yy % 2) * 2 + cc, "orient": xx, "pix": yy // 2}

    def along_first(dx, df):
        return place((x + dx) % XN, (y + swap * df) % YN, (z + core * df) % ZN, core)

    locals_ = [
        pltpu.make_async_copy(counts_in, cnt, loc_sem.at[0]),
        *[
            pltpu.make_async_copy(
                slices_in.at[:, c * 1024 : (c + 1) * 1024], sl.at[:, c * 1024 : (c + 1) * 1024], loc_sem.at[1 + c]
            )
            for c in range(4)
        ],
        pltpu.make_async_copy(owner_in, own_v, loc_sem.at[5]),
        pltpu.make_async_copy(tile_in, til_v, loc_sem.at[6]),
        pltpu.make_async_copy(count_in, pc_v, loc_sem.at[7]),
        pltpu.make_async_copy(old_in, old_v, loc_sem.at[8]),
    ]
    barrier = pltpu.get_barrier_semaphore()
    for d in FAR8:
        pl.semaphore_signal(barrier, inc=1, device_id=place(x, (y + core * d) % YN, (z + swap * d) % ZN, core))
    for dx, df in PLACES[:31]:
        pl.semaphore_signal(barrier, inc=1, device_id=along_first(dx, df))
    for d in FAR4[:3]:
        pl.semaphore_signal(barrier, inc=1, device_id=place((x + d) % XN, y, z, swap))
    pl.semaphore_signal(barrier, inc=1, device_id=place(x, y, z, swap))

    for copy in locals_:
        copy.start()

    locals_[0].wait()
    fit = jnp.zeros((16, 192), F32)
    mass = jnp.zeros((192, 128), F32)
    for c in range(16):
        if c % 4 == 0:
            locals_[1 + c // 4].wait()
        s32 = sl[:, c * 256 : (c + 1) * 256].astype(F32)
        mass = mass + (s32[:, :128] + s32[:, 128:])
        fr = cnt[:, c * 256 : (c + 1) * 256].astype(F32).astype(BF16)
        fit = fit + lax.dot_general(fr, jnp.log(s32).astype(BF16), NT, preferred_element_type=F32)
    fit = fit - lax.dot_general(
        jnp.ones((16, 128), F32), mass, NT, precision=lax.Precision.HIGHEST, preferred_element_type=F32
    )
    fit_scr[...] = jnp.zeros((16, 256), F32)
    fit_scr[:, 0:192] = fit
    lane8 = lanes((8, 128))
    psend[0:16, :] = fit_scr[:, 0:128]
    psend[16:24, :] = jnp.where(lane8 < 64, fit_scr[0:8, 128:256], pltpu.roll(fit_scr[8:16, 128:256], 64, 1))

    pl.semaphore_wait(barrier, 7 + 31 + 3 + 1)

    p_copies = [
        pltpu.make_async_remote_copy(
            psend, precv.at[d - 1], p_send.at[d - 1], p_recv.at[d - 1],
            device_id=place(x, (y + 2 * d) % YN, z, core),
        )
        for d in (2, 1, 3)
    ]
    for copy in p_copies:
        copy.start()
    swap_frames = pltpu.make_async_remote_copy(
        cnt, pcnt, fr_send.at[0], fr_recv.at[0], device_id=place(x, y, z, swap)
    )
    swap_frames.start()

    for copy in locals_[5:]:
        copy.wait()
    tid = til_v[...]
    rid = own_v[...] * 256 + (tid >> 3)
    ry = ((rid >> 1) & 3) * 2 + ((rid >> 6) & 1)
    rz = rid >> 7
    dx = (((rid >> 3) & 3) - x) & 3
    first_step = (ry * swap + rz * core - (y * swap + z * core)) & 7
    second_step = (rz * swap + ry * core - (z * swap + y * core)) & 7
    where_to = dx * 8 + first_step
    spot = jnp.full((32, 192), 31 * 16, jnp.int32)
    for at, (dx, df) in enumerate(PLACES[:31]):
        spot = jnp.where(where_to == dx * 8 + df, at * 16, spot)
    spot = spot + second_step * 2 + (rid & 1)
    spot = jnp.where(((rid >> 5) & 1) == core, spot, -1)
    idpad[...] = jnp.zeros((32, 256), jnp.int32)
    idpad[:, 0:192] = spot
    rowk[0:32, :] = idpad[:, 0:128]
    rowk[32:48, :] = jnp.where(
        lanes((16, 128)) < 64, idpad[0:16, 128:256], pltpu.roll(idpad[16:32, 128:256], 64, 1)
    )
    live = sublanes((32, 192)) + y_hi * 32 < jnp.broadcast_to(pc_v[...], (32, 192))
    shift_rows = jnp.where(live, tid & 7, SHIFTS).astype(F32)
    shift_rows = jnp.concatenate([shift_rows, jnp.full((96, 192), float(SHIFTS), F32)], axis=0)
    eye = (sublanes((192, 192)) == lanes((192, 192))).astype(F32).astype(BF16)
    shm_scr[...] = lax.dot_general(eye, shift_rows.astype(BF16), NT, preferred_element_type=F32)

    def roll_frames(source, half):
        def body(q, _):
            tile = source[:, pl.ds(pl.multiple_of(q * 128, 128), 128)].astype(F32)
            for s in range(SHIFTS):
                moved = pltpu.roll(tile, 17 * s, 1) if s else tile
                grolled[q, half * 128 + s * 16 : half * 128 + (s + 1) * 16, :] = moved.astype(BF16)
            return 0

        lax.fori_loop(0, 32, body, 0, unroll=4)

    def onehot(first, last):
        def body(kb, _):
            line = jnp.broadcast_to(rowk[pl.ds(kb, 1), :], (128, 128))
            for b in range(4):
                hit = line == sublanes((128, 128)) + b * 128
                ohs[b * 128 : (b + 1) * 128, pl.ds(pl.multiple_of(kb * 128, 128), 128)] = jnp.where(
                    hit, 1.0, 0.0
                ).astype(BF16)
            return 0

        lax.fori_loop(first, last, body, 0, unroll=2)

    roll_frames(cnt, 0)
    onehot(0, 48)
    swap_frames.wait_recv()
    roll_frames(pcnt, 1)

    for copy in p_copies:
        copy.wait_recv()
    score = (psend[...] + precv[0] + precv[1] + precv[2]) * (1.0 / math.sqrt(PIXELS))
    score_a, tail = score[0:16], score[16:24]
    off = -3.0e38
    score_b = jnp.concatenate(
        [jnp.where(lane8 < 64, tail, off), jnp.where(lane8 < 64, pltpu.roll(tail, 64, 1), off)], axis=0
    )
    top = jnp.maximum(
        jnp.max(score_a, axis=1, keepdims=True), jnp.max(score_b, axis=1, keepdims=True)
    )
    exp_a = jnp.exp(score_a - top)
    exp_b = jnp.exp(score_b - top)
    total = jnp.sum(exp_a, axis=1, keepdims=True) + jnp.sum(exp_b, axis=1, keepdims=True)
    ssend[0:8, :] = jnp.where(
        lane8 < 64,
        jnp.where(lane8 < 32, top[0:8], total[0:8]),
        jnp.where(lane8 < 96, top[8:16], total[8:16]),
    )
    ssend[8:24, :] = exp_a
    ssend[24:32, :] = jnp.where(lane8 < 64, exp_b[0:8], pltpu.roll(exp_b[8:16], 64, 1))
    s_copies = []
    for d in FAR4[:3]:
        for rel, cc in enumerate((core, swap)):
            slot = (d - 1) * 2 + rel
            s_copies.append(
                pltpu.make_async_remote_copy(
                    ssend.at[0:8], srecv.at[slot], s_send.at[slot], s_recv.at[slot],
                    device_id=place((x + d) % XN, y, z, cc),
                )
            )
    s_copies.append(
        pltpu.make_async_remote_copy(
            ssend, ppart, s_send.at[6], s_recv.at[6], device_id=place(x, y, z, swap)
        )
    )
    for copy in s_copies:
        copy.start()

    s_copies[-1].wait_recv()

    def spread(packed):
        tail = packed[24:32, :]
        tail = jnp.concatenate([tail, pltpu.roll(tail, 64, 1)], axis=0)
        both = jnp.concatenate([packed[8:24, :], tail], axis=1).astype(BF16)
        return [both] * SHIFTS

    eye = (sublanes((192, 256)) == lanes((192, 256))).astype(F32).astype(BF16)
    stack = jnp.concatenate(spread(ssend) + spread(ppart), axis=0)
    rep_scr[...] = lax.dot_general(eye, stack, NT, preferred_element_type=F32).astype(BF16)

    def selections(t4, _):
        columns = pltpu.roll(shm_scr[...], 128 - 4 * t4, 1)
        lane = ((lanes((192, 128)) % 128) // 16).astype(F32).astype(BF16)
        nil = jnp.zeros((192, 128), BF16)
        one = jnp.ones((192, 128), BF16)
        limit = jnp.full((192, 128), SHIFTS, BF16)
        for u in range(4):
            for h in range(2):
                q = t4 * 4 + u + 16 * h
                shift = jnp.broadcast_to(columns[:, u + 16 * h : u + 16 * h + 1], (192, 128)).astype(BF16)
                same = shift == lane
                lhs[q, :, 0:128] = jnp.where(same, rep_scr[:, 0:128], nil)
                lhs[q, :, 128:256] = jnp.where(same, rep_scr[:, 128:256], nil)
                lhs[q, :, 256:384] = jnp.where(shift < limit, one, nil)
        return 0

    lax.fori_loop(0, 4, selections, 0)

    for copy in s_copies[:-1]:
        copy.wait_recv()

    def factors(packed, others):
        stats = packed[0:8, :]
        every = [stats, *others]
        most = functools.reduce(jnp.maximum, every)
        scale = pltpu.roll(jnp.exp(stats - most), 32, 1)
        whole = stats * scale
        for other in others:
            whole = whole + other * pltpu.roll(jnp.exp(other - most), 32, 1)
        factor = scale / whole
        return jnp.broadcast_to(factor[:, 32:33], (8, 128)), jnp.broadcast_to(factor[:, 96:97], (8, 128))

    low, high = factors(ssend, [srecv[0], srecv[2], srecv[4]])
    her_low, her_high = factors(ppart, [srecv[1], srecv[3], srecv[5]])
    column = jnp.concatenate([low, high] * SHIFTS + [her_low, her_high] * SHIFTS, axis=0)
    col_scr[...] = column
    upper = column.astype(BF16).astype(F32)
    parts = jnp.where(lanes((256, 128)) < 64, upper, column - upper).astype(BF16)
    unshifted = jnp.where((lanes((192, 256)) % 128) // 16 == 0, rep_scr[...].astype(F32), 0.0).astype(BF16)
    weights = jnp.dot(unshifted, parts, preferred_element_type=F32)
    weights = weights + pltpu.roll(weights, 64, 1)
    upper = weights.astype(BF16).astype(F32)
    wsel_scr[...] = jnp.where(lanes((192, 128)) < 64, upper, weights - upper).astype(BF16)

    def patches(t4, _):
        for u in range(4):
            t = t4 * 4 + u
            for h in range(2):
                q = t + 16 * h
                scaled = (grolled[q].astype(F32) * col_scr[...]).astype(BF16)
                moved = jnp.dot(lhs[q, :, 0:256], scaled, preferred_element_type=F32).astype(BF16)
                both = jnp.concatenate([moved, lhs[q, :, 256:384] * wsel_scr[...]], axis=1)
                rhs[pl.ds(pl.multiple_of(q * 128, 128), 128), :] = both[0:128]
                rhs[pl.ds(pl.multiple_of(4096 + t * 128 + h * 64, 64), 64), :] = both[128:192]
        return 0

    lax.fori_loop(0, 4, patches, 0)

    diagonal = sublanes((128, 128)) == lanes((128, 128))
    x_copies = []
    for block in range(4):
        total = jnp.dot(ohs[block * 128 : (block + 1) * 128, :], rhs[...], preferred_element_type=F32)
        halves = total[:, 128:256]
        weighed = jnp.where(diagonal, halves + pltpu.roll(halves, 64, 1), 0.0)
        line = jnp.broadcast_to(jnp.sum(weighed, axis=0, keepdims=True), (8, 128))
        for k in range(8):
            xs[block * 8 + k, 0:16, :] = total[k * 16 : (k + 1) * 16, 0:128]
            xs[block * 8 + k, 16:24, :] = pltpu.roll(line, 128 - 16 * k, 1) if k else line
        for at in range(block * 8, min(block * 8 + 8, 31)):
            copy = pltpu.make_async_remote_copy(
                xs.at[at, 0:17], xr.at[at, 0:17], x_send.at[at], x_recv.at[at], device_id=along_first(*PLACES[at])
            )
            copy.start()
            x_copies.append(copy)
    tail = ssend[24:32, :]
    prob_out[:, 0:128] = jnp.concatenate([ssend[8:16, :] * low, ssend[16:24, :] * high], axis=0).astype(BF16)
    prob_out[:, 128:192] = jnp.concatenate([tail * low, pltpu.roll(tail, 64, 1) * high], axis=0)[:, 0:64].astype(BF16)
    brick = xs[31]
    for at, copy in enumerate(x_copies):
        copy.wait_recv()
        brick = brick + xr[at]

    sub8 = sublanes((8, 128))
    for k in range(8):
        tile = brick[8 * (k // 4) : 8 * (k // 4) + 8]
        tile = pltpu.roll(tile, 8 - 2 * (k % 4), 0) if k % 4 else tile
        line = jnp.broadcast_to(brick[16:17], (8, 128))
        line = pltpu.roll(line, 128 - 2 * k, 1) if k else line
        bsd[k] = jnp.where(sub8 < 2, tile, line)
    b_copies = [
        pltpu.make_async_remote_copy(
            bsd.at[d], br.at[d - 1], b_send.at[d - 1], b_recv.at[d - 1],
            device_id=place(x, (y + core * d) % YN, (z + swap * d) % ZN, core),
        )
        for d in FAR8
    ]
    for copy in b_copies:
        copy.start()
    last = bsd[0]
    for d, copy in zip(FAR8, b_copies):
        copy.wait_recv()
        last = last + br[d - 1]
    weight = jnp.sum(jnp.where(lanes((2, 128)) == sublanes((2, 128)), last[2:4], 0.0), axis=1, keepdims=True)
    merged_out[...] = (last[0:2] + PRIOR * old_v[...]) / (weight + PRIOR)

    swap_frames.wait_send()
    for copy in (*p_copies, *s_copies, *x_copies, *b_copies):
        copy.wait_send()


def hand_on(prob_in, merged_in, prob_out, merged_out, sem):
    copies = [pltpu.make_async_copy(prob_in, prob_out, sem.at[0]), pltpu.make_async_copy(merged_in, merged_out, sem.at[1])]
    for copy in copies:
        copy.start()
    for copy in copies:
        copy.wait()


def shards(photon_counts, slices, owner_ids, tile_ids, patch_count, old_model):
    dma = pltpu.SemaphoreType.DMA
    prob, merged = pl.pallas_call(
        kernel,
        out_shape=(jax.ShapeDtypeStruct((16, 192), BF16), jax.ShapeDtypeStruct((2, 128), F32)),
        in_specs=[pl.BlockSpec(memory_space=pl.ANY)] * 6,
        out_specs=(pl.BlockSpec(memory_space=pltpu.VMEM), pl.BlockSpec(memory_space=pltpu.VMEM)),
        scratch_shapes=[
            pltpu.VMEM((16, 4096), jnp.int32),
            pltpu.VMEM((16, 4096), jnp.int32),
            pltpu.VMEM((192, 4096), BF16),
            pltpu.VMEM((32, 192), jnp.int32),
            pltpu.VMEM((32, 192), jnp.int32),
            pltpu.VMEM((1, 192), jnp.int32),
            pltpu.VMEM((2, 128), F32),
            pltpu.VMEM((32, 256), jnp.int32),
            pltpu.VMEM((16, 256), F32),
            pltpu.VMEM((192, 128), F32),
            pltpu.VMEM((192, 256), BF16),
            pltpu.VMEM((192, 128), BF16),
            pltpu.VMEM((256, 128), F32),
            pltpu.VMEM((32, 192, 384), BF16),
            pltpu.VMEM((32, 256, 128), BF16),
            pltpu.VMEM((48, 128), jnp.int32),
            pltpu.VMEM((ROWS, KTOT), BF16),
            pltpu.VMEM((KTOT, 256), BF16),
            pltpu.VMEM((24, 128), F32),
            pltpu.VMEM((3, 24, 128), F32),
            pltpu.VMEM((32, 128), F32),
            pltpu.VMEM((6, 8, 128), F32),
            pltpu.VMEM((32, 128), F32),
            pltpu.VMEM((32, 24, 128), F32),
            pltpu.VMEM((31, 24, 128), F32),
            pltpu.VMEM((8, 8, 128), F32),
            pltpu.VMEM((7, 8, 128), F32),
            dma((9,)),
            dma((1,)), dma((1,)),
            dma((3,)), dma((3,)),
            dma((7,)), dma((7,)),
            dma((31,)), dma((31,)),
            dma((7,)), dma((7,)),
        ],
        compiler_params=pltpu.CompilerParams(
            collective_id=0, has_side_effects=True, vmem_limit_bytes=60 * 1024 * 1024
        ),
        cost_estimate=pl.CostEstimate(flops=2 * 10**9, bytes_accessed=2 * 10**6, transcendentals=10**6),
        name="em_step",
    )(photon_counts, slices, owner_ids.T, tile_ids.T, patch_count.reshape(1, -1), old_model)
    anywhere = pl.BlockSpec(memory_space=pl.ANY)
    return pl.pallas_call(
        hand_on,
        out_shape=(jax.ShapeDtypeStruct((16, 192), BF16), jax.ShapeDtypeStruct((2, 128), F32)),
        in_specs=[anywhere, anywhere],
        out_specs=(anywhere, anywhere),
        scratch_shapes=[dma((2,))],
        compiler_params=pltpu.CompilerParams(vmem_limit_bytes=60 * 1024 * 1024),
        name="hand_on",
    )(prob, merged)


def solution(mesh):
    placed = (
        P("frame", "pix"),
        P("orient", "pix"),
        P("orient", "pix"),
        P("orient", "pix"),
        P("orient"),
        P(("frame", "orient", "pix"), None),
    )
    return jax.shard_map(
        shards,
        mesh=mesh,
        in_specs=placed,
        out_specs=(P("frame", "orient"), P(("frame", "orient", "pix"), None)),
        check_vma=False,
    )
```
